32 devices in a mesh: rows: 16 (over z, y, x), feat: 2 (over core).
Axes of the slice: x: 2, y: 2, z: 4, core: 2. Of those that a mesh axis runs over, the one named last changes fastest.
Arguments:
- features: bfloat16 [12288, 8192], P('rows', 'feat'), may hold values from -400 to 400
- group_index_list: int32 [12288], P('rows'), may hold values from 0 to 511
- threshold_codes: int32 [12288], P('rows'), may hold values from 0 to 3
Outputs:
- counts: float32 [2, 12288], P(None, 'rows')
The draws below stay inside these ranges and needn't reach their ends.
All inputs are finite; a program needn't handle non-finite values.
Results may differ from the reference program's by a relative error of at most 0.00058.
The reference program's roundings to bfloat16 on the way count: a program that leaves them out, or rounds other values in their place, can miss the bound.
Values may be sent and summed in bfloat16 or wider, within the bound.
No kernel may reach another device: no remote copies, remote signals or barrier semaphores. Data moves between devices by JAX's collectives and lax.ppermute only.
A program may use at most 64 MiB of HBM per device.

```python
import math
import jax
import jax.numpy as jnp
from jax import lax

F = 8192
ROWS_DEV = 768
MEET = 3
GROUPS_BLOCK = 32
ROWS = 12288


def group_labels(key):
    blocks = ROWS // ROWS_DEV
    base_key = jax.random.fold_in(key, 11)
    key_ahead, key_member = jax.random.split(base_key)
    row_index = jnp.arange(ROWS, dtype=jnp.int32)
    block_of_row = row_index // ROWS_DEV
    forward_block_count = jax.random.randint(key_ahead, (ROWS,), 0, MEET + 1, dtype=jnp.int32)
    member = jax.random.randint(key_member, (ROWS,), 0, GROUPS_BLOCK, dtype=jnp.int32)
    labels = (block_of_row + forward_block_count) % blocks * GROUPS_BLOCK + member
    maximum_score = blocks * GROUPS_BLOCK - 1
    labels = jnp.where(row_index == ROWS - 1, maximum_score, labels)
    labels = jnp.where(row_index == 0, 0, labels)
    return labels.astype(jnp.int32)


def draw_group_index_list(key, part):
    return group_labels(key)


def draw_features(key, part):
    blocks = ROWS // ROWS_DEV
    labels = group_labels(key)
    key_mix, key_private, key_rowscale, key_colscale, key_dirs = jax.random.split(jax.random.fold_in(key, 23), 5)
    directions = jax.random.normal(key_dirs, (blocks * GROUPS_BLOCK // 2, F), jnp.float32)
    mixing = jax.random.uniform(key_mix, (ROWS, 1), jnp.float32, 0.45, 0.95)
    private = jax.random.normal(key_private, (ROWS, F), jnp.float32)
    row_scale = jnp.exp(jax.random.uniform(key_rowscale, (ROWS, 1), jnp.float32, 0.0, math.log(10.0)))
    col_scale = jnp.exp(jax.random.uniform(key_colscale, (1, F), jnp.float32, 0.0, math.log(10.0)))
    values = mixing * directions[labels // 2] + jnp.sqrt(1.0 - mixing * mixing) * private
    values = jnp.clip(values * row_scale * col_scale, -400.0, 400.0)
    values = values.at[ROWS - 1, 0].set(400.0)
    values = values.at[ROWS - 1, 1].set(-400.0)
    return values.astype(jnp.bfloat16)


def place_ends(drawn, key, smallest, largest):
    index_at = [jax.random.randint(jax.random.fold_in(key, axis), (), 0, length) for axis, length in enumerate(drawn.shape)]
    widest = drawn.shape.index(max(drawn.shape))
    neighbour = index_at[:widest] + [(index_at[widest] + 1) % drawn.shape[widest]] + index_at[widest + 1:]
    return drawn.at[tuple(index_at)].set(smallest).at[tuple(neighbour)].set(largest)


def setup_inputs(seed: int = 0) -> dict:
    seeds = jax.random.split(jax.random.key(seed), 4)
    features = draw_features(jax.random.fold_in(seeds[3], 71), 0)
    group_index_list = draw_group_index_list(jax.random.fold_in(seeds[3], 71), 0)
    threshold_codes = place_ends(jax.random.randint(seeds[2], (ROWS,), 0, 4), jax.random.fold_in(seeds[2], 1), 0, 3).astype(jnp.int32)
    return dict(features=features, group_index_list=group_index_list, threshold_codes=threshold_codes)


SOFTNESS_FACTOR = 0.02

def count_rows(score_matrix, level_codes, own_groups, other_groups):
    cutoff_levels = 0.2 + 0.15 * level_codes.astype(jnp.float32)
    weight_factors = jax.nn.sigmoid((score_matrix - cutoff_levels[:, None]) / SOFTNESS_FACTOR)
    same_group = own_groups[:, None] == other_groups[None, :]
    matched = lax.optimization_barrier(jnp.sum(jnp.where(same_group, weight_factors, 0.0), axis=1))
    overall = lax.optimization_barrier(jnp.sum(weight_factors, axis=1))
    return jnp.stack([matched, overall - matched])

def count_columns(score_matrix, level_codes, own_groups, other_groups):
    cutoff_levels = 0.2 + 0.15 * level_codes.astype(jnp.float32)
    weight_factors = jax.nn.sigmoid((score_matrix - cutoff_levels[None, :]) / SOFTNESS_FACTOR)
    same_group = other_groups[:, None] == own_groups[None, :]
    matched = lax.optimization_barrier(jnp.sum(jnp.where(same_group, weight_factors, 0.0), axis=0))
    overall = lax.optimization_barrier(jnp.sum(weight_factors, axis=0))
    return jnp.stack([matched, overall - matched])

def unit_rows(features):
    widened = features.astype(jnp.float32)
    squares = lax.optimization_barrier(jnp.sum(widened * widened, axis=1))
    inverse = lax.rsqrt(squares / F + 1e-06) / math.sqrt(F)
    return (widened * inverse[:, None]).astype(jnp.bfloat16)

def reference(features, group_index_list, threshold_codes):
    blocks = ROWS // ROWS_DEV
    normed = lax.map(unit_rows, features.reshape(blocks, ROWS_DEV, F))
    groups = group_index_list.reshape(blocks, ROWS_DEV)
    levels = threshold_codes.reshape(blocks, ROWS_DEV)
    counts = jnp.zeros((blocks, 2, ROWS_DEV), jnp.float32)
    for offset in range(1, MEET + 1):

        def meeting(block_index):
            partner = (block_index + offset) % blocks
            score_matrix = jnp.dot(normed[block_index], normed[partner].T, preferred_element_type=jnp.float32)
            local_portion = count_rows(score_matrix, levels[block_index], groups[block_index], groups[partner])
            mirrored = count_columns(score_matrix, levels[partner], groups[partner], groups[block_index])
            return (local_portion, mirrored)
        local_portion, mirrored = lax.map(meeting, jnp.arange(blocks, dtype=jnp.int32))
        counts = counts + local_portion + jnp.roll(mirrored, offset, axis=0)
    return jnp.transpose(counts, (1, 0, 2)).reshape(2, ROWS)
```

```python
import functools
import math

import jax
import jax.numpy as jnp
from jax import lax
from jax.experimental import pallas as pl
from jax.experimental.pallas import tpu as pltpu
from jax.sharding import PartitionSpec as P

MEET = 3
GROUP = MEET + 1
SOFTNESS_FACTOR = 0.02
EPS = 1e-06
SCALE = 32000.0
AXES = ("rows", "feat")
BELOW, OWN = 2, GROUP
SEEN = BELOW + OWN + 1
INNER = ((0, 1), (0, 2), (0, 3), (1, 3), (1, 2), (2, 3))
LOWER = ((-1, 0), (-1, 1), (-1, 2), (-2, 1), (-2, 0))
UPPER = ((4, 1),)
VMEM_LIMIT = 48 * 1024 * 1024


def params():
    return pltpu.CompilerParams(vmem_limit_bytes=VMEM_LIMIT)


def swap(count, mask):
    rows, cores = count
    return [(r * cores + c, (r ^ mask) * cores + c) for r in range(rows) for c in range(cores)]


def ring(count, planes):
    rows, cores = count
    return [
        (r * cores + c, (r + planes * GROUP) % rows * cores + c) for r in range(rows) for c in range(cores)
    ]


def permute(value, pairs):
    return lax.ppermute(value, AXES, pairs)


def prep_kernel(chunks, quarter, full, spot, kept_ref, got_ref, *outs):
    core, me = spot[0], spot[1]
    kept = kept_ref[...].astype(jnp.float32)
    got = got_ref[...].astype(jnp.float32)
    squares = jnp.sum(kept * kept, axis=1, keepdims=True) + jnp.sum(got * got, axis=1, keepdims=True)
    inverse = lax.rsqrt(squares / full + EPS) / math.sqrt(full)
    at = 0
    for mask in range(GROUP):
        start = 0
        for width in chunks:
            columns = pl.ds(pl.multiple_of((me ^ mask) * quarter + start, 128), width)
            mine = (kept_ref[:, columns].astype(jnp.float32) * inverse).astype(jnp.bfloat16)
            other = (got_ref[:, columns].astype(jnp.float32) * inverse).astype(jnp.bfloat16)
            out = outs[at]

            @pl.when(core == 0)
            def _():
                out[:, :width] = mine
                out[:, width:] = other

            @pl.when(core == 1)
            def _():
                out[:, :width] = other
                out[:, width:] = mine

            at += 1
            start += width


def prep(features, got, core, me, chunks, full):
    half, width = got.shape
    step = 32
    steps = half // step
    spot = jnp.stack([core, me]).astype(jnp.int32)
    shapes = [jax.ShapeDtypeStruct((half, 2 * w), jnp.bfloat16) for _ in range(GROUP) for w in chunks]
    outs = pl.pallas_call(
        functools.partial(prep_kernel, chunks, width // GROUP, full),
        grid_spec=pltpu.PrefetchScalarGridSpec(
            num_scalar_prefetch=1,
            grid=(steps,),
            in_specs=[
                pl.BlockSpec((step, width), lambda i, s: (s[0] * steps + i, 0)),
                pl.BlockSpec((step, width), lambda i, s: (i, 0)),
            ],
            out_specs=[pl.BlockSpec((step, s.shape[1]), lambda i, s: (i, 0)) for s in shapes],
        ),
        out_shape=shapes,
        compiler_params=params(),
        name="prep",
    )(spot, features, got)
    count = len(chunks)
    return [outs[m * count : (m + 1) * count] for m in range(GROUP)]


def to_fixed(value):
    return jnp.round(value * SCALE).astype(jnp.int32).astype(jnp.int16)


def from_fixed(value):
    return value.astype(jnp.int32).astype(jnp.float32) * (1.0 / SCALE)


def tile_kernel(count, table, *refs):
    a_refs, own_refs, other_refs = refs[:count], refs[count : 2 * count], refs[2 * count : 3 * count]
    send_x, keep_x, send_y, keep_y = refs[3 * count :]
    tiles = pl.num_programs(0)
    part = keep_x.shape[1]
    contract = (((1,), (1,)), ((), ()))

    def partial_sum(first, b_refs):
        rows = pl.ds(pl.multiple_of(first * part, 16), part)
        total = None
        for a_ref, b_ref in zip(a_refs, b_refs):
            term = lax.dot_general(a_ref[0, rows, :], b_ref[0], contract, preferred_element_type=jnp.float32)
            total = term if total is None else total + term
        return total

    x, y = table[2 * tiles], table[2 * tiles + 1]
    send_x[0] = to_fixed(partial_sum(1 - x, own_refs))
    send_y[0] = to_fixed(partial_sum(1 - y, other_refs))
    keep_x[0] = partial_sum(x, own_refs)
    keep_y[0] = partial_sum(y, other_refs)


def tiles_of(a_chunks, own_chunks, other_chunks, pairs, x, y):
    half = own_chunks[0].shape[1]
    n = len(pairs)
    count = len(own_chunks)
    table = jnp.concatenate(
        [jnp.array([a for a, _ in pairs] + [b for _, b in pairs], jnp.int32), jnp.stack([x, y]).astype(jnp.int32)]
    )
    a_specs = [pl.BlockSpec((1, half, v.shape[2]), lambda t, s: (s[t], 0, 0)) for v in a_chunks]
    b_specs = [pl.BlockSpec((1, half, v.shape[2]), lambda t, s: (s[n + t], 0, 0)) for v in own_chunks]
    out_spec = pl.BlockSpec((1, half // 2, half), lambda t, s: (t, 0, 0))
    sent = jax.ShapeDtypeStruct((n, half // 2, half), jnp.int16)
    held = jax.ShapeDtypeStruct((n, half // 2, half), jnp.float32)
    depth = sum(v.shape[2] for v in own_chunks)
    return pl.pallas_call(
        functools.partial(tile_kernel, count),
        grid_spec=pltpu.PrefetchScalarGridSpec(
            num_scalar_prefetch=1,
            grid=(n,),
            in_specs=a_specs + b_specs + b_specs,
            out_specs=[out_spec] * 4,
        ),
        out_shape=[sent, held, sent, held],
        compiler_params=params(),
        cost_estimate=pl.CostEstimate(
            flops=n * 4 * half * half * depth, bytes_accessed=n * 3 * half * depth * 2, transcendentals=0
        ),
        name="tiles",
    )(table, *a_chunks, *own_chunks, *other_chunks)


def halve_kernel(spot, keep_x, got_x, keep_y, got_y, send_a, hold_a, send_b, hold_b):
    part = send_a.shape[1]
    x, y = spot[0], spot[1]
    for keep, got, bit, send, hold in ((keep_x, got_x, y, send_a, hold_a), (keep_y, got_y, x, send_b, hold_b)):
        away = pl.ds(pl.multiple_of((1 - bit) * part, 16), part)
        here = pl.ds(pl.multiple_of(bit * part, 16), part)
        send[0] = to_fixed(keep[0, away, :] + from_fixed(got[0, away, :]))
        hold[0] = keep[0, here, :] + from_fixed(got[0, here, :])


def halve(keep_x, got_x, keep_y, got_y, x, y):
    n, rows, columns = keep_x.shape
    in_spec = pl.BlockSpec((1, rows, columns), lambda t, s: (t, 0, 0))
    out_spec = pl.BlockSpec((1, rows // 2, columns), lambda t, s: (t, 0, 0))
    sent = jax.ShapeDtypeStruct((n, rows // 2, columns), jnp.int16)
    held = jax.ShapeDtypeStruct((n, rows // 2, columns), jnp.float32)
    return pl.pallas_call(
        halve_kernel,
        grid_spec=pltpu.PrefetchScalarGridSpec(
            num_scalar_prefetch=1, grid=(n,), in_specs=[in_spec] * 4, out_specs=[out_spec] * 4
        ),
        out_shape=[sent, held, sent, held],
        compiler_params=params(),
        name="halve",
    )(jnp.stack([x, y]).astype(jnp.int32), keep_x, got_x, keep_y, got_y)


def count_kernel(table, hold_a, got_a, hold_b, got_b, row_labels, column_labels, row_in, column_in, row_out, column_out):
    t = pl.program_id(0)
    tiles = pl.num_programs(0)
    part = hold_a.shape[1]
    core, x, y = table[2 * tiles], table[2 * tiles + 1], table[2 * tiles + 2]

    @pl.when(t == 0)
    def _():
        row_out[...] = row_in[...]
        column_out[...] = column_in[...]

    a, b = table[t], table[tiles + t]
    for side, hold, got, first, second in ((0, hold_a, got_a, x, y), (1, hold_b, got_b, y, x)):
        rows = pl.ds(pl.multiple_of(((core * 2 + first) * 2 + second) * part, 8), part)
        score = hold[0] + from_fixed(got[0])
        row_level, row_group = row_labels[a, rows, 0:1], row_labels[a, rows, 1:2]
        column_level, column_group = column_labels[b, side, 0:1, :], column_labels[b, side, 1:2, :]
        same = row_group == column_group
        to_row = 1.0 / (1.0 + jnp.exp((row_level - score) * (1.0 / SOFTNESS_FACTOR)))
        to_column = 1.0 / (1.0 + jnp.exp((column_level - score) * (1.0 / SOFTNESS_FACTOR)))
        row_out[a, rows, 0:1] += jnp.sum(jnp.where(same, to_row, 0.0), axis=1, keepdims=True)
        row_out[a, rows, 1:2] += jnp.sum(jnp.where(same, 0.0, to_row), axis=1, keepdims=True)
        column_out[b, side, 0:1, :] += jnp.sum(jnp.where(same, to_column, 0.0), axis=0, keepdims=True)
        column_out[b, side, 1:2, :] += jnp.sum(jnp.where(same, 0.0, to_column), axis=0, keepdims=True)


def count(held, pairs, row_labels, column_labels, row_sums, column_sums, core, x, y):
    hold_a, got_a, hold_b, got_b = held
    n, rows, columns = hold_a.shape
    table = jnp.concatenate(
        [
            jnp.array([a + BELOW for a, _ in pairs] + [b + BELOW for _, b in pairs], jnp.int32),
            jnp.stack([core, x, y]).astype(jnp.int32),
        ]
    )
    tile = pl.BlockSpec((1, rows, columns), lambda t, s: (t, 0, 0))
    whole = [
        pl.BlockSpec(v.shape, functools.partial(lambda nd, t, s: (0,) * nd, v.ndim))
        for v in (row_labels, column_labels, row_sums, column_sums)
    ]
    return pl.pallas_call(
        count_kernel,
        grid_spec=pltpu.PrefetchScalarGridSpec(
            num_scalar_prefetch=1, grid=(n,), in_specs=[tile] * 4 + whole, out_specs=whole[2:]
        ),
        out_shape=[
            jax.ShapeDtypeStruct(row_sums.shape, jnp.float32),
            jax.ShapeDtypeStruct(column_sums.shape, jnp.float32),
        ],
        compiler_params=params(),
        name="count",
    )(table, hold_a, got_a, hold_b, got_b, row_labels, column_labels, row_sums, column_sums)


def local(shape, features, group_index_list, threshold_codes):
    rows_dev, width = features.shape
    full = width * shape[1]
    half = rows_dev // 2
    quarter = width // GROUP
    unit = quarter // 8
    chunks = (2 * unit, 3 * unit, 3 * unit)
    row, core = lax.axis_index("rows"), lax.axis_index("feat")
    me = row % GROUP
    x, y = me % 2, me // 2
    up, down = ring(shape, 1), ring(shape, -1)
    across = [(r * 2 + c, r * 2 + 1 - c) for r in range(shape[0]) for c in range(2)]

    send = lax.dynamic_slice_in_dim(features, (1 - core) * half, half, 0)
    got = permute(send, across)
    parts = prep(features, got, core, me, chunks, full)

    levels = 0.2 + 0.15 * threshold_codes.astype(jnp.float32)
    labels = lax.all_gather(jnp.stack([levels, group_index_list.astype(jnp.float32)]), "rows")
    seen = (row - me - BELOW + jnp.arange(SEEN) + shape[0]) % shape[0]
    labels = labels[seen]
    row_labels = jnp.transpose(labels, (0, 2, 1))
    halves = labels.reshape(SEEN, 2, 2, half).transpose(0, 2, 1, 3)
    column_labels = jnp.where(core == 0, halves, halves[:, ::-1])

    own, other, from_below, from_above = [], [], [], []
    for k in range(len(chunks)):
        got = [parts[0][k]] + [permute(parts[m][k], swap(shape, m)) for m in range(1, GROUP)]

        def block(i):
            inner = jnp.where(x == i % 2, got[0], got[1])
            outer = jnp.where(x == i % 2, got[2], got[3])
            return jnp.where(y == i // 2, inner, outer)

        from_below.append((permute(block(2), up), permute(block(3), up)))
        from_above.append(permute(block(0), down))
        together = jnp.stack([block(i) for i in range(GROUP)])
        own.append(together)
        other.append(permute(together, across))

    below = [jnp.stack(v) for v in from_below]
    above = [v[None] for v in from_above]
    row_sums = jnp.zeros((SEEN, rows_dev, 2), jnp.float32)
    column_sums = jnp.zeros((SEEN, 2, 2, half), jnp.float32)
    for a_chunks, first, pairs in ((own, 0, INNER), (below, -2, LOWER), (above, 4, UPPER)):
        indices = tuple((a - first, b) for a, b in pairs)
        send_x, keep_x, send_y, keep_y = tiles_of(a_chunks, own, other, indices, x, y)
        got_x, got_y = permute(send_x, swap(shape, 1)), permute(send_y, swap(shape, 2))
        send_a, hold_a, send_b, hold_b = halve(keep_x, got_x, keep_y, got_y, x, y)
        got_a, got_b = permute(send_a, swap(shape, 2)), permute(send_b, swap(shape, 1))
        row_sums, column_sums = count(
            (hold_a, got_a, hold_b, got_b), pairs, row_labels, column_labels, row_sums, column_sums, core, x, y
        )

    column_sums = jnp.where(core == 0, column_sums, column_sums[:, ::-1])
    counts = jnp.transpose(row_sums, (0, 2, 1)) + column_sums.transpose(0, 2, 1, 3).reshape(SEEN, 2, rows_dev)
    to_upper = permute(counts[:BELOW], down)
    to_first = permute(counts[SEEN - 1 :], up)
    home = counts[BELOW : BELOW + OWN]
    home = home + jnp.concatenate([to_first, jnp.zeros_like(to_first), to_upper])
    mine = lax.dynamic_index_in_dim(home, me, 0, keepdims=False)
    for m in range(1, GROUP):
        mine = mine + permute(lax.dynamic_index_in_dim(home, me ^ m, 0, keepdims=False), swap(shape, m))
    return mine + permute(mine, across)


def solution(mesh):
    shape = (mesh.shape["rows"], mesh.shape["feat"])
    placed = (P("rows", "feat"), P("rows"), P("rows"))
    return jax.shard_map(
        functools.partial(local, shape), mesh=mesh, in_specs=placed, out_specs=P(None, "rows"), check_vma=False
    )
```

```python
import functools
import math

import jax
import jax.numpy as jnp
from jax import lax
from jax.experimental import pallas as pl
from jax.experimental.pallas import tpu as pltpu
from jax.sharding import PartitionSpec as P

MEET = 3
GROUP = MEET + 1
SOFTNESS_FACTOR = 0.02
EPS = 1e-06
SCALE = 32000.0
AXES = ("rows", "feat")
BELOW, OWN = 2, GROUP
SEEN = BELOW + OWN + 1
INNER = ((0, 1), (0, 2), (0, 3), (1, 3), (1, 2), (2, 3))
LOWER = ((-1, 0), (-1, 1), (-1, 2), (-2, 1), (-2, 0))
UPPER = ((4, 1),)
DIGIT = 64
SHARES = (2, 3, 3)
VMEM_LIMIT = 20 * 1024 * 1024
CONTRACT = (((1,), (1,)), ((), ()))
SHORT = pl.CostEstimate(flops=1, bytes_accessed=1, transcendentals=0)


def params():
    return pltpu.CompilerParams(vmem_limit_bytes=VMEM_LIMIT)


def swap(count, mask):
    rows, cores = count
    return [(r * cores + c, (r ^ mask) * cores + c) for r in range(rows) for c in range(cores)]


def ring(count, planes):
    rows, cores = count
    return [(r * cores + c, (r + planes * GROUP) % rows * cores + c) for r in range(rows) for c in range(cores)]


def permute(value, pairs):
    return lax.ppermute(value, AXES, pairs)


def after(value, *earlier):
    return lax.optimization_barrier((value, *earlier))[0]


def to_fixed(value):
    return jnp.round(value * SCALE).astype(jnp.int32).astype(jnp.int16)


def from_fixed(value):
    return value.astype(jnp.int32).astype(jnp.float32) * (1.0 / SCALE)


def prep_kernel(width, quarter, full, spot, kept_ref, got_ref, inverse_ref, *outs):
    me = spot[2] * 2 + spot[1]
    kept = kept_ref[...].astype(jnp.float32)
    got = got_ref[...].astype(jnp.float32)
    squares = jnp.sum(kept * kept, axis=1, keepdims=True) + jnp.sum(got * got, axis=1, keepdims=True)
    inverse = lax.rsqrt(squares / full + EPS) / math.sqrt(full)
    inverse_ref[...] = jnp.broadcast_to(inverse, inverse_ref.shape)
    for mask, out in enumerate(outs):
        columns = pl.ds(pl.multiple_of((me ^ mask) * quarter, 128), width)
        out[:, :width] = (kept_ref[:, columns].astype(jnp.float32) * inverse).astype(jnp.bfloat16)
        out[:, width:] = (got_ref[:, columns].astype(jnp.float32) * inverse).astype(jnp.bfloat16)


def prep(features, got, spot, width, full):
    half, columns = got.shape
    step = 48 if half % 48 == 0 else 16
    steps = half // step
    shapes = [jax.ShapeDtypeStruct((half, 128), jnp.float32)]
    shapes += [jax.ShapeDtypeStruct((half, 2 * width), jnp.bfloat16)] * GROUP
    return pl.pallas_call(
        functools.partial(prep_kernel, width, columns // GROUP, full),
        grid_spec=pltpu.PrefetchScalarGridSpec(
            num_scalar_prefetch=1,
            grid=(steps,),
            in_specs=[
                pl.BlockSpec((step, columns), lambda i, s: (s[0] * steps + i, 0)),
                pl.BlockSpec((step, columns), lambda i, s: (i, 0)),
            ],
            out_specs=[pl.BlockSpec((step, v.shape[1]), lambda i, s: (i, 0)) for v in shapes],
        ),
        out_shape=shapes,
        compiler_params=params(),
        cost_estimate=SHORT,
        name="prep",
    )(spot, features, got)


def tile_kernel(starts, count, carried, final, table, *refs):
    own_refs, other_refs = refs[:count], refs[count : 2 * count]
    a_refs = refs[2 * count : (-5 if final else -1) - carried]
    total = refs[-1]
    half = total.shape[-2]
    rows = [a_refs[n][0, :half, first : first + ref.shape[2]] for (n, first), ref in zip(starts, own_refs)]
    rows = jnp.concatenate(rows, axis=1)
    own = [ref[0, :half, :] for ref in own_refs]
    other = [ref[0, :half, side] for ref in other_refs for side in halves(ref.shape[2])]
    columns = jnp.concatenate([jnp.concatenate(own, axis=1), jnp.concatenate(other, axis=1)])
    score = lax.dot_general(rows, columns, CONTRACT, preferred_element_type=jnp.float32)
    if carried:
        score = score + refs[-6 if final else -2][0]
    if not final:
        total[0] = score
        return
    total[...] = score
    send_x, keep_x, send_y, keep_y = refs[-5:-1]
    part = half // 2
    at = 2 * pl.num_programs(0)
    x, y = table[at + 1], table[at + 2]
    for first, bit, send, keep in ((0, x, send_x, keep_x), (half, y, send_y, keep_y)):
        columns = pl.ds(first, half)
        send[0] = to_fixed(total[pl.ds(pl.multiple_of((1 - bit) * part, 16), part), columns])
        keep[0] = total[pl.ds(pl.multiple_of(bit * part, 16), part), columns]


def halves(width):
    return slice(width // 2, width), slice(0, width // 2)


def loop(pairs, body):
    if len(pairs) == 1:
        body(0, *pairs[0])
        return
    low = min(min(p) for p in pairs)
    codes = [sum((p[side] - low) << (3 * t) for t, p in enumerate(pairs)) for side in range(2)]

    def step(t, carry):
        a, b = (((jnp.int32(code) >> (3 * t)) & 7) + low for code in codes)
        body(t, a, b)
        return carry

    lax.fori_loop(0, len(pairs), step, 0)


SCALARS = pl.BlockSpec(memory_space=pltpu.SMEM)
WHOLE = pl.BlockSpec(memory_space=pltpu.VMEM)
ANYWHERE = pl.BlockSpec(memory_space=pl.ANY)


def tiles_of(a_arrays, starts, chunks, both, half, pairs, spot, carry=None, final=True):
    n = len(pairs)
    table = jnp.concatenate([jnp.array([a for a, _ in pairs] + [b for _, b in pairs], jnp.int32), spot])
    a_arrays = a_arrays or chunks
    specs = [pl.BlockSpec((1, *v.shape[1:]), lambda t, s: (s[n + t], 0, 0)) for v in (*chunks, *both)]
    specs += [pl.BlockSpec((1, *v.shape[1:]), lambda t, s: (s[t], 0, 0)) for v in a_arrays]
    whole = pl.BlockSpec((1, half, 2 * half), lambda t, s: (t, 0, 0))
    carried = [] if carry is None else [carry]
    specs += [whole] * len(carried)
    sent = jax.ShapeDtypeStruct((n, half // 2, half), jnp.int16)
    held = jax.ShapeDtypeStruct((n, half // 2, half), jnp.float32)
    out_specs = [pl.BlockSpec((1, half // 2, half), lambda t, s: (t, 0, 0))] * 4
    return pl.pallas_call(
        functools.partial(tile_kernel, starts, len(chunks), len(carried), final),
        grid_spec=pltpu.PrefetchScalarGridSpec(
            num_scalar_prefetch=1,
            grid=(n,),
            in_specs=specs,
            out_specs=out_specs if final else whole,
            scratch_shapes=[pltpu.VMEM((half, 2 * half), jnp.float32)] if final else [],
        ),
        out_shape=[sent, held, sent, held] if final else jax.ShapeDtypeStruct((n, half, 2 * half), jnp.float32),
        compiler_params=params(),
        cost_estimate=SHORT,
        name="tiles",
    )(table, *chunks, *both, *a_arrays, *carried)


def arrange_kernel(me, *refs):
    pieces, (together, rising, falling) = refs[:GROUP], refs[GROUP:]
    for m in range(GROUP):
        block = me[0] ^ m
        together[block] = pieces[m][...]

        @pl.when(block >= GROUP - BELOW)
        def _():
            rising[block - (GROUP - BELOW)] = pieces[m][...]

        @pl.when(block == 0)
        def _():
            falling[0] = pieces[m][...]


def arrange(pieces, me):
    rows, width = pieces[0].shape
    step = rows // 2

    def spec(n):
        return pl.BlockSpec((n, step, width), lambda i, s: (0, i, 0))

    counts = (GROUP, BELOW, 1)
    return pl.pallas_call(
        arrange_kernel,
        grid_spec=pltpu.PrefetchScalarGridSpec(
            num_scalar_prefetch=1,
            grid=(rows // step,),
            in_specs=[pl.BlockSpec((step, width), lambda i, s: (i, 0))] * GROUP,
            out_specs=[spec(n) for n in counts],
        ),
        out_shape=[jax.ShapeDtypeStruct((n, rows, width), pieces[0].dtype) for n in counts],
        compiler_params=params(),
        cost_estimate=SHORT,
        name="arrange",
    )(me, *pieces)


def halve_kernel(spot, keep_x, got_x, keep_y, got_y, send_a, hold_a, send_b, hold_b):
    part = send_a.shape[1]
    x, y = spot[1], spot[2]

    def step(t, carry):
        for keep, got, bit, send, hold in ((keep_x, got_x, y, send_a, hold_a), (keep_y, got_y, x, send_b, hold_b)):
            away = pl.ds(pl.multiple_of((1 - bit) * part, 16), part)
            here = pl.ds(pl.multiple_of(bit * part, 16), part)
            send[t] = to_fixed(keep[t, away, :] + from_fixed(got[t, away, :]))
            hold[t] = keep[t, here, :] + from_fixed(got[t, here, :])
        return carry

    lax.fori_loop(0, send_a.shape[0], step, 0)


def halve(keep_x, got_x, keep_y, got_y, spot):
    n, rows, columns = keep_x.shape
    sent = jax.ShapeDtypeStruct((n, rows // 2, columns), jnp.int16)
    held = jax.ShapeDtypeStruct((n, rows // 2, columns), jnp.float32)
    return pl.pallas_call(
        halve_kernel,
        in_specs=[SCALARS] + [WHOLE] * 4,
        out_specs=[WHOLE] * 4,
        out_shape=[sent, held, sent, held],
        compiler_params=params(),
        cost_estimate=SHORT,
        name="halve",
    )(spot, keep_x, got_x, keep_y, got_y)


def slot(block):
    other_plane = (block < 0) | (block >= OWN)
    return ((block + OWN) % GROUP) * 8 + jnp.where(other_plane, 2, 0)


def count_kernel(pairs, first, last, spot, hold_a, got_a, hold_b, got_b, row_labels, column_labels, row_in, column_in, *outs):
    row_out, column_out = outs[-2:] if last else outs
    part = hold_a.shape[1]
    half = column_labels.shape[2] // 2
    core, x, y = spot[0], spot[1], spot[2]
    here = pl.multiple_of(core * half, 128)
    there = pl.multiple_of((1 - core) * half, 128)
    if first:
        row_out[...] = jnp.zeros_like(row_out)
        column_out[...] = jnp.zeros_like(column_out)
    else:
        row_out[...] = row_in[...]
        column_out[...] = column_in[...]
    lanes = lax.broadcasted_iota(jnp.int32, (part, 128), 1)

    def tile(t, a, b):
        to_a, to_b = slot(a), slot(b)
        for side, hold, got, one, two in ((here, hold_a, got_a, x, y), (there, hold_b, got_b, y, x)):
            rows = pl.ds(pl.multiple_of(((core * 2 + one) * 2 + two) * part, 8), part)
            columns = pl.ds(side, half)
            score = hold[t] + from_fixed(got[t])
            row_level, row_group = row_labels[a + BELOW, rows, 0:1], row_labels[a + BELOW, rows, 1:2]
            column_level = column_labels[b + BELOW, 0:1, columns]
            column_group = column_labels[b + BELOW, 1:2, columns]
            same = row_group == column_group
            below = jnp.exp(score * (-1.0 / SOFTNESS_FACTOR))
            to_row = 1.0 / (1.0 + below * jnp.exp(row_level * (1.0 / SOFTNESS_FACTOR)))
            to_column = 1.0 / (1.0 + below * jnp.exp(column_level * (1.0 / SOFTNESS_FACTOR)))
            row_same = jnp.sum(jnp.where(same, to_row, 0.0), axis=1, keepdims=True)
            row_other = jnp.sum(jnp.where(same, 0.0, to_row), axis=1, keepdims=True)
            row_out[rows, :] += jnp.where(lanes == to_a, row_same, jnp.where(lanes == to_a + 1, row_other, 0.0))
            column_same = jnp.sum(jnp.where(same, to_column, 0.0), axis=0, keepdims=True)
            column_other = jnp.sum(jnp.where(same, 0.0, to_column), axis=0, keepdims=True)
            column_out[pl.ds(to_b, 1), columns] += column_same
            column_out[pl.ds(to_b + 1, 1), columns] += column_other

    loop(pairs, tile)
    if last:
        total = jnp.transpose(row_out[...])
        column_out[...] += total[: column_out.shape[0]]
        me = y * 2 + x
        for m in range(GROUP):
            outs[m][...] = column_out[pl.ds(pl.multiple_of((me ^ m) * 8, 8), 8), :]


def count(held, pairs, row_labels, column_labels, sums, last, spot):
    hold_a, got_a, hold_b, got_b = held
    rows_dev = row_labels.shape[1]
    sum_shapes = [
        jax.ShapeDtypeStruct((rows_dev, 128), jnp.float32),
        jax.ShapeDtypeStruct((8 * GROUP, rows_dev), jnp.float32),
    ]
    out_shape = sum_shapes
    scratch = []
    if last:
        out_shape, scratch = [jax.ShapeDtypeStruct((8, rows_dev), jnp.float32)] * GROUP, [
            pltpu.VMEM(v.shape, v.dtype) for v in sum_shapes
        ]
    first = sums is None
    if first:
        sums = [jnp.zeros((8, 128), jnp.float32)] * 2
    return pl.pallas_call(
        functools.partial(count_kernel, pairs, first, last),
        in_specs=[SCALARS] + [WHOLE] * 8,
        out_specs=[WHOLE] * len(out_shape),
        out_shape=out_shape,
        scratch_shapes=scratch,
        compiler_params=params(),
        cost_estimate=SHORT,
        name="count",
    )(spot, hold_a, got_a, hold_b, got_b, row_labels, column_labels, *sums)


def local(shape, features, group_index_list, threshold_codes):
    rows_dev, width = features.shape
    full = width * shape[1]
    half = rows_dev // 2
    quarter = width // GROUP
    chunks = tuple(n * quarter // 8 for n in SHARES)
    firsts = tuple(sum(chunks[:k]) for k in range(len(chunks)))
    row, core = lax.axis_index("rows"), lax.axis_index("feat")
    me = row % GROUP
    x, y = me % 2, me // 2
    spot = jnp.stack([core, x, y]).astype(jnp.int32)
    up, down = ring(shape, 1), ring(shape, -1)
    across = [(r * 2 + c, r * 2 + 1 - c) for r in range(shape[0]) for c in range(2)]

    got = permute(lax.dynamic_slice_in_dim(features, (1 - core) * half, half, 0), across)
    inverse, *pieces = prep(features, got, spot, chunks[0], full)
    inverse = inverse[:, :1]

    lanes = 2 * chunks[1]
    extra = -(-3 * rows_dev // (lanes * 16)) * 16
    labels = jnp.concatenate([group_index_list // DIGIT, group_index_list % DIGIT, threshold_codes])
    labels = jnp.pad(labels, (0, extra * lanes - 3 * rows_dev)).astype(jnp.bfloat16).reshape(extra, lanes)

    def part(mask, k):
        first = (me ^ mask) * quarter + firsts[k]
        cuts = [lax.dynamic_slice(v, (r, first), (half, chunks[k])) for v, r in ((features, core * half), (got, 0))]
        cut = jnp.concatenate([(v.astype(jnp.float32) * inverse).astype(jnp.bfloat16) for v in cuts], axis=1)
        return jnp.concatenate([cut, labels]) if k == 1 else cut

    parts = [pieces] + [[part(m, k) for m in range(GROUP)] for k in range(1, len(chunks))]
    blocks, both, falling, from_below, from_above, got, earlier = [], [], [], [], [], [], []
    last = len(chunks) - 1
    plain = tuple((k, 0) for k in range(last))
    for k in range(len(chunks)):
        ready = [[v] for v in got] if got else [[]] * GROUP
        got = [
            permute(after(parts[k][m], *ready[m - 1], *from_below[max(k - 2, 0) : max(k - 1, 0)]), swap(shape, m))
            for m in range(1, GROUP)
        ]
        waits = [p for later in parts[1:] for p in later] if k == 0 else [*earlier, both[-1]]
        if k == last:
            inner_sum = tiles_of(None, plain, blocks, both, half, INNER, spot, final=False)
            waits.append(inner_sum)
        pieces = [after(v, *waits) for v in (parts[k][0], *got)]
        together, rising, sinking = arrange(pieces, me.reshape(1))
        blocks.append(together)
        falling.append(sinking)
        from_below.append(permute(after(rising, *earlier), up))
        both.append(permute(together, across))
        if k == 0:
            from_above.append(permute(after(sinking, both[0]), down))
        if k == 1:
            labels_above = permute(after(sinking[:, half:], both[1]), down)
        earlier = [from_below[-1], *(from_above if k == 0 else (labels_above,))]

    seen = jnp.concatenate([from_below[1][:, half:], blocks[1][:, half:], labels_above])
    seen = seen.astype(jnp.float32).reshape(SEEN, -1)[:, : 3 * rows_dev].reshape(SEEN, 3, rows_dev)
    column_labels = jnp.stack([0.2 + 0.15 * seen[:, 2], seen[:, 0] * DIGIT + seen[:, 1]], axis=1)
    row_labels = jnp.transpose(column_labels, (0, 2, 1))
    rest = jnp.concatenate([v[:, :half] for v in falling[1:]], axis=2)
    from_above.append(permute(after(rest, from_below[-1], column_labels, row_labels), down))

    def reduce_x_y(tiles, *earlier):
        send_x, keep_x, send_y, keep_y = tiles
        got_x = permute(after(send_x, *earlier), swap(shape, 1))
        got_y = permute(after(send_y, *earlier), swap(shape, 2))
        return keep_x, got_x, keep_y, got_y

    def reduce_y_x(send_a, hold_a, send_b, hold_b):
        return hold_a, permute(send_a, swap(shape, 2)), hold_b, permute(send_b, swap(shape, 1))

    def tally(held, pairs, sums):
        return count(held, pairs, row_labels, column_labels, sums, pairs is UPPER, spot)

    lower = tuple((a + BELOW, b) for a, b in LOWER)
    upper = tuple((a - OWN, b) for a, b in UPPER)
    one = ((0, 0),)
    tiles = tiles_of([blocks[last]], one, [blocks[last]], [both[last]], half, INNER, spot, carry=inner_sum)
    inner = reduce_x_y(tiles)
    below = [after(v, tiles[0], tiles[2]) for v in from_below[:last]]
    lower_sum = tiles_of(below, plain, blocks[:last], both[:last], half, lower, spot, final=False)
    tiles = tiles_of(from_below[last:], one, blocks[last:], both[last:], half, lower, spot, carry=lower_sum)
    lower_held = reduce_x_y(tiles, inner[1], inner[3])
    inner = reduce_y_x(*halve(*inner, spot))
    lower_held = reduce_y_x(*halve(*lower_held, spot))
    starts = ((0, 0),) + tuple((1, 2 * (firsts[k] - firsts[1])) for k in range(1, len(chunks)))
    upper_held = reduce_x_y(tiles_of(from_above, starts, blocks, both, half, upper, spot))
    sums = tally(inner, INNER, None)
    sums = tally(lower_held, LOWER, sums)
    upper_held = reduce_y_x(*halve(*upper_held, spot))
    sums = tally(upper_held, UPPER, sums)

    mine = sums[0]
    for m in range(1, GROUP):
        mine = mine + permute(sums[m], swap(shape, m))
    home = []
    for r in range(shape[0]):
        block = r % GROUP
        if block in (0, GROUP - 2, GROUP - 1):
            planes = 1 if block == 0 else -1
            home += [(r * 2 + c, (r + planes * GROUP) % shape[0] * 2 + c) for c in range(2)]
    mine = mine[:2] + permute(mine[2:4], home)
    return mine + permute(mine, across)


def solution(mesh):
    shape = (mesh.shape["rows"], mesh.shape["feat"])
    placed = (P("rows", "feat"), P("rows"), P("rows"))
    return jax.shard_map(
        functools.partial(local, shape), mesh=mesh, in_specs=placed, out_specs=P(None, "rows"), check_vma=False
    )
```

```python
import functools
import math

import jax
import jax.numpy as jnp
from jax import lax
from jax.experimental import pallas as pl
from jax.experimental.pallas import tpu as pltpu
from jax.sharding import PartitionSpec as P

MEET = 3
GROUP = MEET + 1
SOFTNESS_FACTOR = 0.02
EPS = 1e-06
SCALE = 32000.0
AXES = ("rows", "feat")
BELOW, OWN = 2, GROUP
SEEN = BELOW + OWN + 1
INNER = ((0, 1), (0, 2), (0, 3), (1, 3), (1, 2), (2, 3))
NEAR = ((-1, 0), (-1, 1), (-1, 2))
FAR = ((-2, 1), (-2, 0))
UPPER = ((4, 1),)
DIGIT = 64
SHARES = (2, 3, 3)
EARLY = (0,)
EARLIER = 2
CONTRACT = (((1,), (1,)), ((), ()))
SHORT = pl.CostEstimate(flops=1, bytes_accessed=1, transcendentals=0)


def params(mib=10):
    return pltpu.CompilerParams(vmem_limit_bytes=mib * 1024 * 1024)


def swap(count, mask):
    rows, cores = count
    return [(r * cores + c, (r ^ mask) * cores + c) for r in range(rows) for c in range(cores)]


def ring(count, planes):
    rows, cores = count
    return [(r * cores + c, (r + planes * GROUP) % rows * cores + c) for r in range(rows) for c in range(cores)]


def permute(value, pairs):
    return lax.ppermute(value, AXES, pairs)


def in_hbm(value):
    return pltpu.with_memory_space_constraint(value, pltpu.HBM)


def after(value, *earlier):
    return lax.optimization_barrier((value, *earlier))[0]


def to_fixed(value):
    return jnp.round(value * SCALE).astype(jnp.int32)


def added(one, two):
    return one.astype(jnp.int32) + two.astype(jnp.int32)


def tile_kernel(starts, count, carried, final, direct, table, *refs):
    own_refs, other_refs = refs[:count], refs[count : 2 * count]
    a_refs = refs[2 * count : (-5 if final else -1) - carried]
    total = refs[-1]
    half = total.shape[-2]
    rows = [a_refs[n][0, :half, first : first + ref.shape[2]] for (n, first), ref in zip(starts, own_refs)]
    rows = jnp.concatenate(rows, axis=1)
    own = [ref[0, :half, :] for ref in own_refs]
    other = [ref[0, :half, side] for ref in other_refs for side in halves(ref.shape[2])]
    columns = jnp.concatenate([jnp.concatenate(own, axis=1), jnp.concatenate(other, axis=1)])
    score = lax.dot_general(rows, columns, CONTRACT, preferred_element_type=jnp.float32)
    score = to_fixed(score)
    if carried:
        score = added(score, refs[-6 if final else -2][0])
    if not final:
        total[0] = score.astype(jnp.int16)
        return
    total[...] = score
    send_x, keep_x, send_y, keep_y = refs[-5:-1]
    part = half // 2
    at = 2 * pl.num_programs(0)
    x, y = table[at + 1], table[at + 2]
    if direct:
        part = part // 2
        for mask, out in enumerate(refs[-5:-1]):
            owner = (x ^ (mask & 1)) * 2 + (y ^ (mask >> 1))
            out[0] = total[pl.ds(pl.multiple_of(owner * part, 16), part), :].astype(jnp.int16)
        return
    for first, bit, send, keep in ((0, x, send_x, keep_x), (half, y, send_y, keep_y)):
        columns = pl.ds(first, half)
        send[0] = total[pl.ds(pl.multiple_of((1 - bit) * part, 16), part), columns].astype(jnp.int16)
        keep[0] = total[pl.ds(pl.multiple_of(bit * part, 16), part), columns].astype(jnp.int16)


def halves(width):
    return slice(width // 2, width), slice(0, width // 2)


def loop(pairs, body):
    if len(pairs) == 1:
        body(0, *pairs[0])
        return
    low = min(min(p) for p in pairs)
    codes = [sum((p[side] - low) << (3 * t) for t, p in enumerate(pairs)) for side in range(2)]

    def step(t, carry):
        a, b = (((jnp.int32(code) >> (3 * t)) & 7) + low for code in codes)
        body(t, a, b)
        return carry

    lax.fori_loop(0, len(pairs), step, 0)


SCALARS = pl.BlockSpec(memory_space=pltpu.SMEM)
WHOLE = pl.BlockSpec(memory_space=pltpu.VMEM)
ANYWHERE = pl.BlockSpec(memory_space=pl.ANY)


def tiles_of(a_arrays, starts, chunks, both, half, pairs, spot, carry=None, skip=0, final=True, direct=False):
    n = len(pairs)
    table = jnp.concatenate([jnp.array([a for a, _ in pairs] + [b for _, b in pairs], jnp.int32), spot])
    a_arrays = [in_hbm(v) for v in a_arrays] if a_arrays else chunks
    specs = [pl.BlockSpec((1, *v.shape[1:]), lambda t, s: (s[n + t], 0, 0)) for v in (*chunks, *both)]
    specs += [pl.BlockSpec((1, *v.shape[1:]), lambda t, s: (s[t], 0, 0)) for v in a_arrays]
    whole = pl.BlockSpec((1, half, 2 * half), lambda t, s: (t, 0, 0))
    depth = sum(v.shape[2] for v in chunks)
    carried = [] if carry is None else [carry]
    specs += [pl.BlockSpec((1, half, 2 * half), lambda t, s: (skip + t, 0, 0))] * len(carried)
    sent = pltpu.HBM((n, half // 2, half), jnp.int16)
    held = jax.ShapeDtypeStruct((n, half // 2, half), jnp.int16)
    out_specs = [pl.BlockSpec((1, half // 2, half), lambda t, s: (t, 0, 0))] * 4
    outs = [sent, held, sent, held]
    if direct:
        out_specs = [pl.BlockSpec((1, half // 4, 2 * half), lambda t, s: (t, 0, 0))] * 4
        held, sent = (f((n, half // 4, 2 * half), jnp.int16) for f in (jax.ShapeDtypeStruct, pltpu.HBM))
        outs = [held, sent, sent, sent]
    return pl.pallas_call(
        functools.partial(tile_kernel, starts, len(chunks), len(carried), final, direct),
        grid_spec=pltpu.PrefetchScalarGridSpec(
            num_scalar_prefetch=1,
            grid=(n,),
            in_specs=specs,
            out_specs=out_specs if final else whole,
            scratch_shapes=[pltpu.VMEM((half, 2 * half), jnp.int32)] if final else [],
        ),
        out_shape=outs if final else jax.ShapeDtypeStruct((n, half, 2 * half), jnp.int16),
        compiler_params=params(8 + depth // 192),
        cost_estimate=SHORT if final else pl.CostEstimate(flops=n * 4 * half * half * depth, bytes_accessed=n * 6 * half * depth, transcendentals=0),
        name="tiles",
    )(table, *chunks, *both, *a_arrays, *carried)


def arrange_kernel(me, *refs):
    pieces, (together, rising, falling) = refs[:GROUP], refs[GROUP:]
    for m in range(GROUP):
        block = me[0] ^ m
        together[block] = pieces[m][...]

        @pl.when(block >= GROUP - BELOW)
        def _():
            rising[block - (GROUP - BELOW)] = pieces[m][...]

        @pl.when(block == 0)
        def _():
            falling[0] = pieces[m][...]


def arrange(pieces, me):
    rows, width = pieces[0].shape
    step = rows // 2

    def spec(n):
        return pl.BlockSpec((n, step, width), lambda i, s: (0, i, 0))

    counts = (GROUP, BELOW, 1)
    return pl.pallas_call(
        arrange_kernel,
        grid_spec=pltpu.PrefetchScalarGridSpec(
            num_scalar_prefetch=1,
            grid=(rows // step,),
            in_specs=[pl.BlockSpec((step, width), lambda i, s: (i, 0))] * GROUP,
            out_specs=[spec(n) for n in counts],
        ),
        out_shape=[jax.ShapeDtypeStruct((GROUP, rows, width), pieces[0].dtype)]
        + [pltpu.HBM((n, rows, width), pieces[0].dtype) for n in counts[1:]],
        compiler_params=params(),
        cost_estimate=SHORT,
        name="arrange",
    )(me, *pieces)


def halve_kernel(spot, keep_x, got_x, keep_y, got_y, send_a, hold_a, send_b, hold_b):
    part = send_a.shape[1]
    x, y = spot[1], spot[2]

    def step(t, carry):
        for keep, got, bit, send, hold in ((keep_x, got_x, y, send_a, hold_a), (keep_y, got_y, x, send_b, hold_b)):
            away = pl.ds(pl.multiple_of((1 - bit) * part, 16), part)
            here = pl.ds(pl.multiple_of(bit * part, 16), part)
            send[t] = added(keep[t, away, :], got[t, away, :]).astype(jnp.int16)
            hold[t] = added(keep[t, here, :], got[t, here, :]).astype(jnp.int16)
        return carry

    lax.fori_loop(0, send_a.shape[0], step, 0)


def halve(keep_x, got_x, keep_y, got_y, spot):
    n, rows, columns = keep_x.shape
    sent = held = jax.ShapeDtypeStruct((n, rows // 2, columns), jnp.int16)
    return pl.pallas_call(
        halve_kernel,
        in_specs=[SCALARS] + [WHOLE] * 4,
        out_specs=[WHOLE] * 4,
        out_shape=[sent, held, sent, held],
        compiler_params=params(),
        cost_estimate=SHORT,
        name="halve",
    )(spot, keep_x, got_x, keep_y, got_y)


def labels_kernel(seen, row_labels, column_labels):
    rows_dev = seen.shape[2]
    lines = []
    for block in range(SEEN):
        high, low, code = (seen[block, i : i + 1, :].astype(jnp.float32) for i in range(3))
        level, group = 0.2 + 0.15 * code, high * DIGIT + low
        column_labels[block, 0:1, :] = level
        column_labels[block, 1:2, :] = group
        lines += [level, group]
    lines.append(jnp.zeros((128 - 2 * SEEN, rows_dev), jnp.float32))
    row_labels[...] = jnp.transpose(jnp.concatenate(lines))


def labels_of(seen):
    rows_dev = seen.shape[2]
    return pl.pallas_call(
        labels_kernel,
        in_specs=[WHOLE],
        out_specs=[WHOLE] * 2,
        out_shape=[
            jax.ShapeDtypeStruct((rows_dev, 128), jnp.float32),
            jax.ShapeDtypeStruct((SEEN, 2, rows_dev), jnp.float32),
        ],
        compiler_params=params(),
        cost_estimate=SHORT,
        name="labels",
    )(seen)


def slot(block):
    other_plane = (block < 0) | (block >= OWN)
    return ((block + OWN) % GROUP) * 8 + jnp.where(other_plane, 2, 0)


def count_kernel(pairs, first, last, spot, *refs):
    held, (row_labels, column_labels, row_in, column_in), outs = refs[:4], refs[4:8], refs[8:]
    row_out, column_out = outs[-2:] if last else outs
    part = held[0].shape[1]
    half = column_labels.shape[2] // 2
    core, x, y = spot[0], spot[1], spot[2]
    here = pl.multiple_of(core * half, 128)
    there = pl.multiple_of((1 - core) * half, 128)
    if first:
        row_out[...] = jnp.zeros_like(row_out)
        column_out[...] = jnp.zeros_like(column_out)
    else:
        row_out[...] = row_in[...]
        column_out[...] = column_in[...]
    lanes = lax.broadcasted_iota(jnp.int32, (part, 128), 1)

    def tile(t, a, b):
        to_a, to_b = slot(a), slot(b)
        for at, side, one, two in ((0, here, x, y), (1, there, x if last else y, y if last else x)):
            rows = pl.ds(pl.multiple_of(((core * 2 + one) * 2 + two) * part, 8), part)
            columns = pl.ds(side, half)
            if last:
                share = pl.ds(at * half, half)
                score = added(held[0][t, :, share], held[1][t, :, share])
                score += added(held[2][t, :, share], held[3][t, :, share])
            else:
                score = added(held[2 * at][t], held[2 * at + 1][t])
            score = score.astype(jnp.float32) * (1.0 / SCALE)
            labels = row_labels[rows, :]
            lane = 2 * (a + BELOW)
            row_level = jnp.sum(jnp.where(lanes == lane, labels, 0.0), axis=1, keepdims=True)
            row_group = jnp.sum(jnp.where(lanes == lane + 1, labels, 0.0), axis=1, keepdims=True)
            column_level = column_labels[b + BELOW, 0:1, columns]
            column_group = column_labels[b + BELOW, 1:2, columns]
            same = row_group == column_group
            below = jnp.exp(score * (-1.0 / SOFTNESS_FACTOR))
            to_row = 1.0 / (1.0 + below * jnp.exp(row_level * (1.0 / SOFTNESS_FACTOR)))
            to_column = 1.0 / (1.0 + below * jnp.exp(column_level * (1.0 / SOFTNESS_FACTOR)))
            row_same = jnp.sum(jnp.where(same, to_row, 0.0), axis=1, keepdims=True)
            row_other = jnp.sum(jnp.where(same, 0.0, to_row), axis=1, keepdims=True)
            row_out[rows, :] += jnp.where(lanes == to_a, row_same, jnp.where(lanes == to_a + 1, row_other, 0.0))
            column_same = jnp.sum(jnp.where(same, to_column, 0.0), axis=0, keepdims=True)
            column_other = jnp.sum(jnp.where(same, 0.0, to_column), axis=0, keepdims=True)
            column_out[pl.ds(to_b, 1), columns] += column_same
            column_out[pl.ds(to_b + 1, 1), columns] += column_other

    loop(pairs, tile)
    if last:
        total = jnp.transpose(row_out[...])
        column_out[...] += total[: column_out.shape[0]]
        me = y * 2 + x
        for m in range(GROUP):
            outs[m][...] = column_out[pl.ds(pl.multiple_of((me ^ m) * 8, 8), 8), :]


def count(held, pairs, row_labels, column_labels, sums, last, spot):
    rows_dev = row_labels.shape[0]
    sum_shapes = [
        jax.ShapeDtypeStruct((rows_dev, 128), jnp.float32),
        jax.ShapeDtypeStruct((8 * GROUP, rows_dev), jnp.float32),
    ]
    out_shape = sum_shapes
    scratch = []
    if last:
        out_shape, scratch = [jax.ShapeDtypeStruct((8, rows_dev), jnp.float32)] * GROUP, [
            pltpu.VMEM(v.shape, v.dtype) for v in sum_shapes
        ]
    first = sums is None
    if first:
        sums = [jnp.zeros((8, 128), jnp.float32)] * 2
    return pl.pallas_call(
        functools.partial(count_kernel, pairs, first, last),
        in_specs=[SCALARS] + [WHOLE] * 8,
        out_specs=[WHOLE] * len(out_shape),
        out_shape=out_shape,
        scratch_shapes=scratch,
        compiler_params=params(),
        cost_estimate=SHORT,
        name="count",
    )(spot, *held, row_labels, column_labels, *sums)


def local(shape, features, group_index_list, threshold_codes):
    rows_dev, width = features.shape
    full = width * shape[1]
    half = rows_dev // 2
    quarter = width // GROUP
    chunks = tuple(n * quarter // 8 for n in SHARES)
    firsts = tuple(sum(chunks[:k]) for k in range(len(chunks)))
    row, core = lax.axis_index("rows"), lax.axis_index("feat")
    me = row % GROUP
    x, y = me % 2, me // 2
    spot = jnp.stack([core, x, y]).astype(jnp.int32)
    up, down = ring(shape, 1), ring(shape, -1)
    across = [(r * 2 + c, r * 2 + 1 - c) for r in range(shape[0]) for c in range(2)]

    got = permute(lax.dynamic_slice_in_dim(features, (1 - core) * half, half, 0), across)
    widened = features.astype(jnp.float32)
    squares = lax.psum(jnp.sum(widened * widened, axis=1), "feat")
    inverse = lax.rsqrt(squares / full + EPS) / math.sqrt(full)
    inverse = lax.dynamic_slice_in_dim(inverse, core * half, half, 0)[:, None]

    lanes = 2 * chunks[1]
    extra = -(-3 * rows_dev // (lanes * 16)) * 16
    labels = jnp.concatenate([group_index_list // DIGIT, group_index_list % DIGIT, threshold_codes])
    labels = jnp.pad(labels, (0, extra * lanes - 3 * rows_dev)).astype(jnp.bfloat16).reshape(extra, lanes)

    def part(mask, k):
        first = (me ^ mask) * quarter + firsts[k]
        cuts = [lax.dynamic_slice(v, (r, first), (half, chunks[k])) for v, r in ((features, core * half), (got, 0))]
        cut = jnp.concatenate([(v.astype(jnp.float32) * inverse).astype(jnp.bfloat16) for v in cuts], axis=1)
        return jnp.concatenate([cut, labels]) if k == 1 else cut

    parts = [[part(m, k) for m in range(GROUP)] for k in range(len(chunks))]
    blocks, both, falling, from_below, from_above, got, earlier = [], [], [], [], [], [], []
    last = len(chunks) - 1
    near, far = (tuple((a + BELOW, b) for a, b in pairs) for pairs in (NEAR, FAR))
    plain = tuple((k, 0) for k in range(last))
    for k in range(len(chunks)):
        ready = [*got] if got else [None] * (GROUP - 1)
        got = [
            permute(after(parts[k][m], *ready[m - 1 : m][: k], *from_below[max(k - 2, 0) : max(k - 1, 0)]), swap(shape, m))
            for m in range(1, GROUP)
        ]
        waits = [p for later in parts[1:] for p in later] if k == 0 else [*earlier, both[-1]]
        if k == last:
            inner_sum = tiles_of(None, plain[:EARLIER], blocks[:EARLIER], both[:EARLIER], half, INNER, spot, final=False)
            waits.append(inner_sum)
        pieces = [after(v, *waits) for v in (parts[k][0], *got)]
        together, rising, sinking = arrange(pieces, me.reshape(1))
        blocks.append(together)
        falling.append(sinking)
        from_below.append(permute(after(rising, *earlier), up))
        both.append(permute(together, across))
        earlier = [from_below[-1]]
        if k in EARLY:
            from_above.append(permute(after(sinking[:, :half], both[k]), down))
            earlier.append(from_above[-1])
        if k == 1:
            labels_above = permute(after(sinking[:, half:], both[1]), down)
            earlier.append(labels_above)

    def reduce_x_y(tiles, *earlier):
        send_x, keep_x, send_y, keep_y = tiles
        got_x = permute(after(send_x, *earlier), swap(shape, 1))
        got_y = permute(after(send_y, *earlier), swap(shape, 2))
        return keep_x, got_x, keep_y, got_y

    def reduce_y_x(send_a, hold_a, send_b, hold_b):
        return hold_a, permute(send_a, swap(shape, 2)), hold_b, permute(send_b, swap(shape, 1))

    def tally(held, pairs, sums):
        return count(held, pairs, row_labels, column_labels, sums, pairs is UPPER, spot)

    upper = tuple((a - OWN, b) for a, b in UPPER)
    one = ((0, 0),)
    rest = tuple((k, 0) for k in range(len(chunks) - EARLIER))
    tiles = tiles_of(None, rest, blocks[EARLIER:], both[EARLIER:], half, INNER, spot, carry=inner_sum)
    inner = reduce_x_y(tiles)
    below = [after(v, tiles[0], tiles[2]) for v in from_below[:last]]
    plain = tuple((k, 0) for k in range(last))
    lower_sum = tiles_of(below, plain, blocks[:last], both[:last], half, near + far, spot, final=False)
    seen = jnp.concatenate([from_below[1][:, half:], blocks[1][:, half:], labels_above])
    seen = after(seen, *tiles).reshape(SEEN, -1)[:, : 3 * rows_dev].reshape(SEEN, 3, rows_dev)
    row_labels, column_labels = labels_of(seen)
    late = [k for k in range(len(chunks)) if k not in EARLY]
    falling = jnp.concatenate([falling[k][:, :half] for k in late], axis=2)
    from_above.append(permute(after(falling, lower_sum, column_labels, row_labels), down))

    one = ((0, 0),)
    ends = (blocks[last:], both[last:], half)
    near_below = [after(from_below[last], tiles[0], tiles[2])]
    tiles = tiles_of(near_below, one, *ends, near, spot, carry=lower_sum)
    near_held = reduce_x_y(tiles, inner[1], inner[3])
    far_below = [after(from_below[last], tiles[0], tiles[2])]
    far_held = reduce_x_y(tiles_of(far_below, one, *ends, far, spot, carry=lower_sum, skip=len(NEAR)), inner[1], inner[3])
    inner = reduce_y_x(*halve(*inner, spot))
    near_held = reduce_y_x(*halve(*near_held, spot))
    far_held = reduce_y_x(*halve(*far_held, spot))
    begins = {k: 2 * sum(chunks[i] for i in late if i < k) for k in late}
    starts = tuple((EARLY.index(k), 0) if k in EARLY else (len(EARLY), begins[k]) for k in range(len(chunks)))
    keep, *sends = tiles_of(from_above, starts, blocks, both, half, upper, spot, direct=True)
    upper_held = [keep] + [permute(v, swap(shape, m)) for m, v in enumerate(sends, 1)]
    sums = tally(inner, INNER, None)
    sums = tally(near_held, NEAR, sums)
    sums = tally(far_held, FAR, sums)
    sums = tally(upper_held, UPPER, sums)

    mine = sums[0]
    for m in range(1, GROUP):
        mine = mine + permute(sums[m], swap(shape, m))
    home = []
    for r in range(shape[0]):
        block = r % GROUP
        if block in (0, GROUP - 2, GROUP - 1):
            planes = 1 if block == 0 else -1
            home += [(r * 2 + c, (r + planes * GROUP) % shape[0] * 2 + c) for c in range(2)]
    mine = mine[:2] + permute(mine[2:4], home)
    return mine + permute(mine, across)


def solution(mesh):
    shape = (mesh.shape["rows"], mesh.shape["feat"])
    placed = (P("rows", "feat"), P("rows"), P("rows"))
    return jax.shard_map(
        functools.partial(local, shape), mesh=mesh, in_specs=placed, out_specs=P(None, "rows"), check_vma=False
    )
```

```python
import functools
import math

import jax
import jax.numpy as jnp
from jax import lax
from jax.experimental import pallas as pl
from jax.experimental.pallas import tpu as pltpu
from jax.sharding import PartitionSpec as P

MEET = 3
GROUP = MEET + 1
SOFTNESS_FACTOR = 0.02
EPS = 1e-06
SCALE = 32000.0
AXES = ("rows", "feat")
BELOW, OWN = 2, GROUP
SEEN = BELOW + OWN + 1
INNER = ((0, 1), (0, 2), (0, 3), (1, 3), (1, 2), (2, 3))
NEAR = ((-1, 0), (-1, 1), (-1, 2))
FAR = ((-2, 1), (-2, 0))
UPPER = ((4, 1),)
DIGIT = 64
SHARES = (2, 3, 3)
EARLY = (0,)
EARLIER = 2
CONTRACT = (((1,), (1,)), ((), ()))
SHORT = pl.CostEstimate(flops=1, bytes_accessed=1, transcendentals=0)


def params(mib=10):
    return pltpu.CompilerParams(vmem_limit_bytes=mib * 1024 * 1024)


def swap(count, mask):
    rows, cores = count
    return [(r * cores + c, (r ^ mask) * cores + c) for r in range(rows) for c in range(cores)]


def ring(count, planes):
    rows, cores = count
    return [(r * cores + c, (r + planes * GROUP) % rows * cores + c) for r in range(rows) for c in range(cores)]


def permute(value, pairs):
    return lax.ppermute(value, AXES, pairs)


def in_hbm(value):
    return pltpu.with_memory_space_constraint(value, pltpu.HBM)


def after(value, *earlier):
    return lax.optimization_barrier((value, *earlier))[0]


def to_fixed(value):
    return jnp.round(value * SCALE).astype(jnp.int32)


def added(one, two):
    return one.astype(jnp.int32) + two.astype(jnp.int32)


def tile_kernel(starts, count, carried, final, direct, table, *refs):
    own_refs, other_refs = refs[:count], refs[count : 2 * count]
    a_refs = refs[2 * count : (-5 if final else -1) - carried]
    total = refs[-1]
    half = total.shape[-2]
    rows = [a_refs[n][0, :half, first : first + ref.shape[2]] for (n, first), ref in zip(starts, own_refs)]
    rows = jnp.concatenate(rows, axis=1)
    own = [ref[0, :half, :] for ref in own_refs]
    other = [ref[0, :half, side] for ref in other_refs for side in halves(ref.shape[2])]
    columns = jnp.concatenate([jnp.concatenate(own, axis=1), jnp.concatenate(other, axis=1)])
    score = lax.dot_general(rows, columns, CONTRACT, preferred_element_type=jnp.float32)
    score = to_fixed(score)
    if carried:
        score = added(score, refs[-6 if final else -2][0])
    if not final:
        total[0] = score.astype(jnp.int16)
        return
    total[...] = score
    send_x, keep_x, send_y, keep_y = refs[-5:-1]
    part = half // 2
    at = 2 * pl.num_programs(0)
    x, y = table[at + 1], table[at + 2]
    if direct:
        part = part // 2
        for mask, out in enumerate(refs[-5:-1]):
            owner = (x ^ (mask & 1)) * 2 + (y ^ (mask >> 1))
            out[0] = total[pl.ds(pl.multiple_of(owner * part, 16), part), :].astype(jnp.int16)
        return
    for first, bit, send, keep in ((0, x, send_x, keep_x), (half, y, send_y, keep_y)):
        columns = pl.ds(first, half)
        send[0] = total[pl.ds(pl.multiple_of((1 - bit) * part, 16), part), columns].astype(jnp.int16)
        keep[0] = total[pl.ds(pl.multiple_of(bit * part, 16), part), columns].astype(jnp.int16)


def halves(width):
    return slice(width // 2, width), slice(0, width // 2)


def loop(pairs, body):
    if len(pairs) == 1:
        body(0, *pairs[0])
        return
    low = min(min(p) for p in pairs)
    codes = [sum((p[side] - low) << (3 * t) for t, p in enumerate(pairs)) for side in range(2)]

    def step(t, carry):
        a, b = (((jnp.int32(code) >> (3 * t)) & 7) + low for code in codes)
        body(t, a, b)
        return carry

    lax.fori_loop(0, len(pairs), step, 0)


SCALARS = pl.BlockSpec(memory_space=pltpu.SMEM)
WHOLE = pl.BlockSpec(memory_space=pltpu.VMEM)
ANYWHERE = pl.BlockSpec(memory_space=pl.ANY)


def tiles_of(a_arrays, starts, chunks, both, half, pairs, spot, carry=None, skip=0, final=True, direct=False):
    n = len(pairs)
    table = jnp.concatenate([jnp.array([a for a, _ in pairs] + [b for _, b in pairs], jnp.int32), spot])
    a_arrays = [in_hbm(v) for v in a_arrays] if a_arrays else chunks
    specs = [pl.BlockSpec((1, *v.shape[1:]), lambda t, s: (s[n + t], 0, 0)) for v in (*chunks, *both)]
    specs += [pl.BlockSpec((1, *v.shape[1:]), lambda t, s: (s[t], 0, 0)) for v in a_arrays]
    whole = pl.BlockSpec((1, half, 2 * half), lambda t, s: (t, 0, 0))
    depth = sum(v.shape[2] for v in chunks)
    carried = [] if carry is None else [carry]
    specs += [pl.BlockSpec((1, half, 2 * half), lambda t, s: (skip + t, 0, 0))] * len(carried)
    sent = pltpu.HBM((n, half // 2, half), jnp.int16)
    held = pltpu.HBM((n, half // 2, half), jnp.int16)
    out_specs = [pl.BlockSpec((1, half // 2, half), lambda t, s: (t, 0, 0))] * 4
    outs = [sent, held, sent, held]
    if direct:
        out_specs = [pl.BlockSpec((1, half // 4, 2 * half), lambda t, s: (t, 0, 0))] * 4
        held, sent = (f((n, half // 4, 2 * half), jnp.int16) for f in (jax.ShapeDtypeStruct, pltpu.HBM))
        outs = [held, sent, sent, sent]
    return pl.pallas_call(
        functools.partial(tile_kernel, starts, len(chunks), len(carried), final, direct),
        grid_spec=pltpu.PrefetchScalarGridSpec(
            num_scalar_prefetch=1,
            grid=(n,),
            in_specs=specs,
            out_specs=out_specs if final else whole,
            scratch_shapes=[pltpu.VMEM((half, 2 * half), jnp.int32)] if final else [],
        ),
        out_shape=outs if final else jax.ShapeDtypeStruct((n, half, 2 * half), jnp.int16),
        compiler_params=params(8 + depth // 192),
        cost_estimate=SHORT if final else pl.CostEstimate(flops=n * 4 * half * half * depth, bytes_accessed=n * 6 * half * depth, transcendentals=0),
        name="tiles",
    )(table, *chunks, *both, *a_arrays, *carried)


def arrange_kernel(me, *refs):
    pieces, (together, rising, falling) = refs[:GROUP], refs[GROUP:]
    for m in range(GROUP):
        block = me[0] ^ m
        together[block] = pieces[m][...]

        @pl.when(block >= GROUP - BELOW)
        def _():
            rising[block - (GROUP - BELOW)] = pieces[m][...]

        @pl.when(block == 0)
        def _():
            falling[0] = pieces[m][...]


def arrange(pieces, me):
    rows, width = pieces[0].shape
    step = max(n for n in range(16, rows // 2 + 1, 16) if rows % n == 0)

    def spec(n):
        return pl.BlockSpec((n, step, width), lambda i, s: (0, i, 0))

    counts = (GROUP, BELOW, 1)
    return pl.pallas_call(
        arrange_kernel,
        grid_spec=pltpu.PrefetchScalarGridSpec(
            num_scalar_prefetch=1,
            grid=(rows // step,),
            in_specs=[pl.BlockSpec((step, width), lambda i, s: (i, 0))] * GROUP,
            out_specs=[spec(n) for n in counts],
        ),
        out_shape=[jax.ShapeDtypeStruct((GROUP, rows, width), pieces[0].dtype)]
        + [pltpu.HBM((n, rows, width), pieces[0].dtype) for n in counts[1:]],
        compiler_params=params(),
        cost_estimate=SHORT,
        name="arrange",
    )(me, *pieces)


def halve_kernel(spot, keep_x, got_x, keep_y, got_y, send_a, hold_a, send_b, hold_b):
    part = send_a.shape[1]
    x, y = spot[1], spot[2]

    def step(t, carry):
        for keep, got, bit, send, hold in ((keep_x, got_x, y, send_a, hold_a), (keep_y, got_y, x, send_b, hold_b)):
            away = pl.ds(pl.multiple_of((1 - bit) * part, 16), part)
            here = pl.ds(pl.multiple_of(bit * part, 16), part)
            send[t] = added(keep[t, away, :], got[t, away, :]).astype(jnp.int16)
            hold[t] = added(keep[t, here, :], got[t, here, :]).astype(jnp.int16)
        return carry

    lax.fori_loop(0, send_a.shape[0], step, 0)


def halve(keep_x, got_x, keep_y, got_y, spot):
    n, rows, columns = keep_x.shape
    sent = held = jax.ShapeDtypeStruct((n, rows // 2, columns), jnp.int16)
    return pl.pallas_call(
        halve_kernel,
        in_specs=[SCALARS] + [WHOLE] * 4,
        out_specs=[WHOLE] * 4,
        out_shape=[sent, held, sent, held],
        compiler_params=params(),
        cost_estimate=SHORT,
        name="halve",
    )(spot, keep_x, got_x, keep_y, got_y)


def labels_kernel(seen, row_labels, column_labels):
    rows_dev = seen.shape[2]
    lines = []
    for block in range(SEEN):
        high, low, code = (seen[block, i : i + 1, :].astype(jnp.float32) for i in range(3))
        level, group = 0.2 + 0.15 * code, high * DIGIT + low
        column_labels[block, 0:1, :] = level
        column_labels[block, 1:2, :] = group
        lines += [level, group]
    lines.append(jnp.zeros((128 - 2 * SEEN, rows_dev), jnp.float32))
    row_labels[...] = jnp.transpose(jnp.concatenate(lines))


def labels_of(seen):
    rows_dev = seen.shape[2]
    return pl.pallas_call(
        labels_kernel,
        in_specs=[WHOLE],
        out_specs=[WHOLE] * 2,
        out_shape=[
            jax.ShapeDtypeStruct((rows_dev, 128), jnp.float32),
            jax.ShapeDtypeStruct((SEEN, 2, rows_dev), jnp.float32),
        ],
        compiler_params=params(),
        cost_estimate=SHORT,
        name="labels",
    )(seen)


def slot(block):
    other_plane = (block < 0) | (block >= OWN)
    return ((block + OWN) % GROUP) * 8 + jnp.where(other_plane, 2, 0)


def count_kernel(pairs, first, last, spot, *refs):
    held, (row_labels, column_labels, row_in, column_in), outs = refs[:4], refs[4:8], refs[8:]
    row_out, column_out = outs[-2:] if last else outs
    part = held[0].shape[1]
    half = column_labels.shape[2] // 2
    core, x, y = spot[0], spot[1], spot[2]
    here = pl.multiple_of(core * half, 128)
    there = pl.multiple_of((1 - core) * half, 128)
    if first:
        row_out[...] = jnp.zeros_like(row_out)
        column_out[...] = jnp.zeros_like(column_out)
    else:
        row_out[...] = row_in[...]
        column_out[...] = column_in[...]
    lanes = lax.broadcasted_iota(jnp.int32, (part, 128), 1)

    def tile(t, a, b):
        to_a, to_b = slot(a), slot(b)
        for at, side, one, two in ((0, here, x, y), (1, there, x if last else y, y if last else x)):
            rows = pl.ds(pl.multiple_of(((core * 2 + one) * 2 + two) * part, 8), part)
            columns = pl.ds(side, half)
            if last:
                share = pl.ds(at * half, half)
                score = added(held[0][t, :, share], held[1][t, :, share])
                score += added(held[2][t, :, share], held[3][t, :, share])
            else:
                score = added(held[2 * at][t], held[2 * at + 1][t])
            score = score.astype(jnp.float32) * (1.0 / SCALE)
            labels = row_labels[rows, :]
            lane = 2 * (a + BELOW)
            row_level = jnp.sum(jnp.where(lanes == lane, labels, 0.0), axis=1, keepdims=True)
            row_group = jnp.sum(jnp.where(lanes == lane + 1, labels, 0.0), axis=1, keepdims=True)
            column_level = column_labels[b + BELOW, 0:1, columns]
            column_group = column_labels[b + BELOW, 1:2, columns]
            same = row_group == column_group
            below = jnp.exp(score * (-1.0 / SOFTNESS_FACTOR))
            to_row = 1.0 / (1.0 + below * jnp.exp(row_level * (1.0 / SOFTNESS_FACTOR)))
            to_column = 1.0 / (1.0 + below * jnp.exp(column_level * (1.0 / SOFTNESS_FACTOR)))
            row_same = jnp.sum(jnp.where(same, to_row, 0.0), axis=1, keepdims=True)
            row_other = jnp.sum(jnp.where(same, 0.0, to_row), axis=1, keepdims=True)
            row_out[rows, :] += jnp.where(lanes == to_a, row_same, jnp.where(lanes == to_a + 1, row_other, 0.0))
            column_same = jnp.sum(jnp.where(same, to_column, 0.0), axis=0, keepdims=True)
            column_other = jnp.sum(jnp.where(same, 0.0, to_column), axis=0, keepdims=True)
            column_out[pl.ds(to_b, 1), columns] += column_same
            column_out[pl.ds(to_b + 1, 1), columns] += column_other

    loop(pairs, tile)
    if last:
        total = jnp.transpose(row_out[...])
        column_out[...] += total[: column_out.shape[0]]
        me = y * 2 + x
        for m in range(GROUP):
            outs[m][...] = column_out[pl.ds(pl.multiple_of((me ^ m) * 8, 8), 8), :]


def count(held, pairs, row_labels, column_labels, sums, last, spot):
    rows_dev = row_labels.shape[0]
    sum_shapes = [
        jax.ShapeDtypeStruct((rows_dev, 128), jnp.float32),
        jax.ShapeDtypeStruct((8 * GROUP, rows_dev), jnp.float32),
    ]
    out_shape = sum_shapes
    scratch = []
    if last:
        out_shape, scratch = [jax.ShapeDtypeStruct((8, rows_dev), jnp.float32)] * GROUP, [
            pltpu.VMEM(v.shape, v.dtype) for v in sum_shapes
        ]
    first = sums is None
    if first:
        sums = [jnp.zeros((8, 128), jnp.float32)] * 2
    return pl.pallas_call(
        functools.partial(count_kernel, pairs, first, last),
        in_specs=[SCALARS] + [WHOLE] * 8,
        out_specs=[WHOLE] * len(out_shape),
        out_shape=out_shape,
        scratch_shapes=scratch,
        compiler_params=params(),
        cost_estimate=SHORT,
        name="count",
    )(spot, *held, row_labels, column_labels, *sums)


def local(shape, features, group_index_list, threshold_codes):
    rows_dev, width = features.shape
    full = width * shape[1]
    half = rows_dev // 2
    quarter = width // GROUP
    chunks = tuple(n * quarter // 8 for n in SHARES)
    firsts = tuple(sum(chunks[:k]) for k in range(len(chunks)))
    row, core = lax.axis_index("rows"), lax.axis_index("feat")
    me = row % GROUP
    x, y = me % 2, me // 2
    spot = jnp.stack([core, x, y]).astype(jnp.int32)
    up, down = ring(shape, 1), ring(shape, -1)
    across = [(r * 2 + c, r * 2 + 1 - c) for r in range(shape[0]) for c in range(2)]

    given = [
        lax.dynamic_slice(features, ((1 - core) * half, q * quarter), (half, chunks[0])) for q in range(GROUP)
    ]
    soon = permute(jnp.concatenate(given, axis=1), across)
    widened = features.astype(jnp.float32)
    squares = lax.psum(jnp.sum(widened * widened, axis=1), "feat")
    got = permute(after(features, squares, soon), across)
    inverse = lax.rsqrt(squares / full + EPS) / math.sqrt(full)
    inverse = lax.dynamic_slice_in_dim(inverse, core * half, half, 0)[:, None]

    lanes = 2 * chunks[1]
    extra = -(-3 * rows_dev // (lanes * 16)) * 16
    labels = jnp.concatenate([group_index_list // DIGIT, group_index_list % DIGIT, threshold_codes])
    labels = jnp.pad(labels, (0, extra * lanes - 3 * rows_dev)).astype(jnp.bfloat16).reshape(extra, lanes)

    def part(mask, k):
        first = (me ^ mask) * quarter + firsts[k]
        cut = lax.dynamic_slice(features, (core * half, first), (half, chunks[k]))
        if k == 0:
            other = lax.dynamic_slice_in_dim(soon, (me ^ mask) * chunks[0], chunks[0], 1)
        else:
            other = lax.dynamic_slice(got, (core * half, first), (half, chunks[k]))
        cuts = (cut, other)
        cut = jnp.concatenate([(v.astype(jnp.float32) * inverse).astype(jnp.bfloat16) for v in cuts], axis=1)
        return jnp.concatenate([cut, labels]) if k == 1 else cut

    parts = [[part(m, k) for m in range(GROUP)] for k in range(len(chunks))]
    blocks, both, falling, from_below, from_above, got, earlier = [], [], [], [], [], [], []
    last = len(chunks) - 1
    near, far = (tuple((a + BELOW, b) for a, b in pairs) for pairs in (NEAR, FAR))
    plain = tuple((k, 0) for k in range(last))
    for k in range(len(chunks)):
        ready = [*got] if got else [None] * (GROUP - 1)
        got = [
            permute(after(parts[k][m], *ready[m - 1 : m][: k], *from_below[max(k - 2, 0) : max(k - 1, 0)]), swap(shape, m))
            for m in range(1, GROUP)
        ]
        waits = [p for later in parts[1:] for p in later] if k == 0 else [*earlier, both[-1]]
        if k == last:
            inner_sum = tiles_of(None, plain[:EARLIER], blocks[:EARLIER], both[:EARLIER], half, INNER, spot, final=False)
            waits.append(inner_sum)
        pieces = [after(v, *waits) for v in (parts[k][0], *got)]
        together, rising, sinking = arrange(pieces, me.reshape(1))
        blocks.append(together)
        falling.append(sinking)
        from_below.append(permute(after(rising, *earlier), up))
        both.append(permute(together, across))
        earlier = [from_below[-1]]
        if k in EARLY:
            from_above.append(permute(after(sinking[:, :half], both[k]), down))
            earlier.append(from_above[-1])
        if k == 1:
            labels_above = permute(after(sinking[:, half:], both[1]), down)
            earlier.append(labels_above)

    def reduce_x_y(tiles, *earlier):
        send_x, keep_x, send_y, keep_y = tiles
        got_x = permute(after(send_x, *earlier), swap(shape, 1))
        got_y = permute(after(send_y, *earlier), swap(shape, 2))
        return keep_x, got_x, keep_y, got_y

    def reduce_y_x(send_a, hold_a, send_b, hold_b):
        return hold_a, permute(send_a, swap(shape, 2)), hold_b, permute(send_b, swap(shape, 1))

    def tally(held, pairs, sums):
        return count(held, pairs, row_labels, column_labels, sums, pairs is UPPER, spot)

    upper = tuple((a - OWN, b) for a, b in UPPER)
    one = ((0, 0),)
    rest = tuple((k, 0) for k in range(len(chunks) - EARLIER))
    tiles = tiles_of(None, rest, blocks[EARLIER:], both[EARLIER:], half, INNER, spot, carry=inner_sum)
    inner = reduce_x_y(tiles)
    below = [after(v, tiles[0], tiles[2]) for v in from_below[:last]]
    plain = tuple((k, 0) for k in range(last))
    lower_sum = tiles_of(below, plain, blocks[:last], both[:last], half, near + far, spot, final=False)
    seen = jnp.concatenate([from_below[1][:, half:], blocks[1][:, half:], labels_above])
    seen = after(seen, *tiles).reshape(SEEN, -1)[:, : 3 * rows_dev].reshape(SEEN, 3, rows_dev)
    row_labels, column_labels = labels_of(seen)
    late = [k for k in range(len(chunks)) if k not in EARLY]
    falling = [after(v, tiles[0], tiles[2]) for v in falling]
    falling = jnp.concatenate([falling[k][:, :half] for k in late], axis=2)
    from_above.append(permute(after(falling, lower_sum, column_labels, row_labels), down))

    one = ((0, 0),)
    ends = (blocks[last:], both[last:], half)
    near_below = [after(from_below[last], tiles[0], tiles[2])]
    tiles = tiles_of(near_below, one, *ends, near, spot, carry=lower_sum)
    near_held = reduce_x_y(tiles, inner[1], inner[3])
    far_below = [after(from_below[last], tiles[0], tiles[2])]
    far_held = reduce_x_y(tiles_of(far_below, one, *ends, far, spot, carry=lower_sum, skip=len(NEAR)), inner[1], inner[3])
    inner = reduce_y_x(*halve(*inner, spot))
    near_held = reduce_y_x(*halve(*near_held, spot))
    far_held = reduce_y_x(*halve(*far_held, spot))
    begins = {k: 2 * sum(chunks[i] for i in late if i < k) for k in late}
    starts = tuple((EARLY.index(k), 0) if k in EARLY else (len(EARLY), begins[k]) for k in range(len(chunks)))
    keep, *sends = tiles_of(from_above, starts, blocks, both, half, upper, spot, direct=True)
    upper_held = [keep] + [permute(v, swap(shape, m)) for m, v in enumerate(sends, 1)]
    sums = tally(inner, INNER, None)
    sums = tally(near_held, NEAR, sums)
    sums = tally(far_held, FAR, sums)
    sums = tally(upper_held, UPPER, sums)

    mine = sums[0]
    for m in range(1, GROUP):
        mine = mine + permute(sums[m], swap(shape, m))
    home = []
    for r in range(shape[0]):
        block = r % GROUP
        if block in (0, GROUP - 2, GROUP - 1):
            planes = 1 if block == 0 else -1
            home += [(r * 2 + c, (r + planes * GROUP) % shape[0] * 2 + c) for c in range(2)]
    mine = mine[:2] + permute(mine[2:4], home)
    return mine + permute(mine, across)


def solution(mesh):
    shape = (mesh.shape["rows"], mesh.shape["feat"])
    placed = (P("rows", "feat"), P("rows"), P("rows"))
    return jax.shard_map(
        functools.partial(local, shape), mesh=mesh, in_specs=placed, out_specs=P(None, "rows"), check_vma=False
    )
```

```python
import functools
import math

import jax
import jax.numpy as jnp
from jax import lax
from jax.experimental import pallas as pl
from jax.experimental.pallas import tpu as pltpu
from jax.sharding import PartitionSpec as P

MEET = 3
GROUP = MEET + 1
SOFTNESS_FACTOR = 0.02
EPS = 1e-06
SCALE = 32000.0
AXES = ("rows", "feat")
BELOW, OWN = 2, GROUP
SEEN = BELOW + OWN + 1
INNER = ((0, 1), (0, 2), (0, 3), (1, 3), (1, 2), (2, 3))
NEAR = ((-1, 0), (-1, 1), (-1, 2))
FAR = ((-2, 1), (-2, 0))
UPPER = ((4, 1),)
DIGIT = 64
SHARES = (2, 3, 3)
EARLY = (0,)
EARLIER = 2
CONTRACT = (((1,), (1,)), ((), ()))
SHORT = pl.CostEstimate(flops=1, bytes_accessed=1, transcendentals=0)


def params(mib=10):
    return pltpu.CompilerParams(vmem_limit_bytes=mib * 1024 * 1024)


def swap(count, mask):
    rows, cores = count
    return [(r * cores + c, (r ^ mask) * cores + c) for r in range(rows) for c in range(cores)]


def ring(count, planes):
    rows, cores = count
    return [(r * cores + c, (r + planes * GROUP) % rows * cores + c) for r in range(rows) for c in range(cores)]


def permute(value, pairs):
    return lax.ppermute(value, AXES, pairs)


def in_hbm(value):
    return pltpu.with_memory_space_constraint(value, pltpu.HBM)


def after(value, *earlier):
    return lax.optimization_barrier((value, *earlier))[0]


def to_fixed(value):
    return jnp.round(value * SCALE).astype(jnp.int32)


def added(one, two):
    return one.astype(jnp.int32) + two.astype(jnp.int32)


def tile_kernel(starts, count, carried, final, direct, table, *refs):
    own_refs, other_refs = refs[:count], refs[count : 2 * count]
    a_refs = refs[2 * count : (-5 if final else -1) - carried]
    total = refs[-1]
    half = total.shape[-2]
    rows = [a_refs[n][0, :half, first : first + ref.shape[2]] for (n, first), ref in zip(starts, own_refs)]
    rows = jnp.concatenate(rows, axis=1)
    own = [ref[0, :half, :] for ref in own_refs]
    other = [ref[0, :half, side] for ref in other_refs for side in halves(ref.shape[2])]
    columns = jnp.concatenate([jnp.concatenate(own, axis=1), jnp.concatenate(other, axis=1)])
    score = lax.dot_general(rows, columns, CONTRACT, preferred_element_type=jnp.float32)
    score = to_fixed(score)
    if carried:
        score = added(score, refs[-6 if final else -2][0])
    if not final:
        total[0] = score.astype(jnp.int16)
        return
    total[...] = score
    send_x, keep_x, send_y, keep_y = refs[-5:-1]
    part = half // 2
    at = 2 * pl.num_programs(0)
    x, y = table[at + 1], table[at + 2]
    if direct:
        part = part // 2
        for mask, out in enumerate(refs[-5:-1]):
            owner = (x ^ (mask & 1)) * 2 + (y ^ (mask >> 1))
            out[0] = total[pl.ds(pl.multiple_of(owner * part, 16), part), :].astype(jnp.int16)
        return
    for first, bit, send, keep in ((0, x, send_x, keep_x), (half, y, send_y, keep_y)):
        columns = pl.ds(first, half)
        send[0] = total[pl.ds(pl.multiple_of((1 - bit) * part, 16), part), columns].astype(jnp.int16)
        keep[0] = total[pl.ds(pl.multiple_of(bit * part, 16), part), columns].astype(jnp.int16)


def halves(width):
    return slice(width // 2, width), slice(0, width // 2)


def loop(pairs, body):
    if len(pairs) == 1:
        body(0, *pairs[0])
        return
    low = min(min(p) for p in pairs)
    codes = [sum((p[side] - low) << (3 * t) for t, p in enumerate(pairs)) for side in range(2)]

    def step(t, carry):
        a, b = (((jnp.int32(code) >> (3 * t)) & 7) + low for code in codes)
        body(t, a, b)
        return carry

    lax.fori_loop(0, len(pairs), step, 0)


SCALARS = pl.BlockSpec(memory_space=pltpu.SMEM)
WHOLE = pl.BlockSpec(memory_space=pltpu.VMEM)
ANYWHERE = pl.BlockSpec(memory_space=pl.ANY)


def tiles_of(a_arrays, starts, chunks, both, half, pairs, spot, carry=None, skip=0, final=True, direct=False):
    n = len(pairs)
    table = jnp.concatenate([jnp.array([a for a, _ in pairs] + [b for _, b in pairs], jnp.int32), spot])
    a_arrays = [in_hbm(v) for v in a_arrays] if a_arrays else chunks
    specs = [pl.BlockSpec((1, *v.shape[1:]), lambda t, s: (s[n + t], 0, 0)) for v in (*chunks, *both)]
    specs += [pl.BlockSpec((1, *v.shape[1:]), lambda t, s: (s[t], 0, 0)) for v in a_arrays]
    whole = pl.BlockSpec((1, half, 2 * half), lambda t, s: (t, 0, 0))
    depth = sum(v.shape[2] for v in chunks)
    carried = [] if carry is None else [carry]
    specs += [pl.BlockSpec((1, half, 2 * half), lambda t, s: (skip + t, 0, 0))] * len(carried)
    sent = pltpu.HBM((n, half // 2, half), jnp.int16)
    held = pltpu.HBM((n, half // 2, half), jnp.int16)
    out_specs = [pl.BlockSpec((1, half // 2, half), lambda t, s: (t, 0, 0))] * 4
    outs = [sent, held, sent, held]
    if direct:
        out_specs = [pl.BlockSpec((1, half // 4, 2 * half), lambda t, s: (t, 0, 0))] * 4
        held, sent = (f((n, half // 4, 2 * half), jnp.int16) for f in (jax.ShapeDtypeStruct, pltpu.HBM))
        outs = [held, sent, sent, sent]
    return pl.pallas_call(
        functools.partial(tile_kernel, starts, len(chunks), len(carried), final, direct),
        grid_spec=pltpu.PrefetchScalarGridSpec(
            num_scalar_prefetch=1,
            grid=(n,),
            in_specs=specs,
            out_specs=out_specs if final else whole,
            scratch_shapes=[pltpu.VMEM((half, 2 * half), jnp.int32)] if final else [],
        ),
        out_shape=outs if final else jax.ShapeDtypeStruct((n, half, 2 * half), jnp.int16),
        compiler_params=params(8 + depth // 192),
        cost_estimate=SHORT if final else pl.CostEstimate(flops=n * 4 * half * half * depth, bytes_accessed=n * 6 * half * depth, transcendentals=0),
        name="tiles",
    )(table, *chunks, *both, *a_arrays, *carried)


def arrange_kernel(me, *refs):
    pieces, (together, rising, falling) = refs[:GROUP], refs[GROUP:]
    for m in range(GROUP):
        block = me[0] ^ m
        together[block] = pieces[m][...]

        @pl.when(block >= GROUP - BELOW)
        def _():
            rising[block - (GROUP - BELOW)] = pieces[m][...]

        @pl.when(block == 0)
        def _():
            falling[0] = pieces[m][...]


def arrange(pieces, me):
    rows, width = pieces[0].shape
    high, wide = (rows // 2, width) if rows % 32 == 0 else (rows, width // 2)

    def place(i):
        return (i, 0) if high < rows else (0, i)

    counts = (GROUP, BELOW, 1)
    return pl.pallas_call(
        arrange_kernel,
        grid_spec=pltpu.PrefetchScalarGridSpec(
            num_scalar_prefetch=1,
            grid=(2,),
            in_specs=[pl.BlockSpec((high, wide), lambda i, s: place(i))] * GROUP,
            out_specs=[pl.BlockSpec((n, high, wide), lambda i, s: (0, *place(i))) for n in counts],
        ),
        out_shape=[jax.ShapeDtypeStruct((GROUP, rows, width), pieces[0].dtype)]
        + [pltpu.HBM((n, rows, width), pieces[0].dtype) for n in counts[1:]],
        compiler_params=params(),
        cost_estimate=SHORT,
        name="arrange",
    )(me, *pieces)


def halve_kernel(spot, keep_x, got_x, keep_y, got_y, send_a, hold_a, send_b, hold_b):
    part = send_a.shape[1]
    x, y = spot[1], spot[2]

    def step(t, carry):
        for keep, got, bit, send, hold in ((keep_x, got_x, y, send_a, hold_a), (keep_y, got_y, x, send_b, hold_b)):
            away = pl.ds(pl.multiple_of((1 - bit) * part, 16), part)
            here = pl.ds(pl.multiple_of(bit * part, 16), part)
            send[t] = added(keep[t, away, :], got[t, away, :]).astype(jnp.int16)
            hold[t] = added(keep[t, here, :], got[t, here, :]).astype(jnp.int16)
        return carry

    lax.fori_loop(0, send_a.shape[0], step, 0)


def halve(keep_x, got_x, keep_y, got_y, spot):
    n, rows, columns = keep_x.shape
    sent = held = jax.ShapeDtypeStruct((n, rows // 2, columns), jnp.int16)
    return pl.pallas_call(
        halve_kernel,
        in_specs=[SCALARS] + [WHOLE] * 4,
        out_specs=[WHOLE] * 4,
        out_shape=[sent, held, sent, held],
        compiler_params=params(),
        cost_estimate=SHORT,
        name="halve",
    )(spot, keep_x, got_x, keep_y, got_y)


def labels_kernel(seen, row_labels, column_labels):
    rows_dev = seen.shape[2]
    lines = []
    for block in range(SEEN):
        high, low, code = (seen[block, i : i + 1, :].astype(jnp.float32) for i in range(3))
        level, group = 0.2 + 0.15 * code, high * DIGIT + low
        column_labels[block, 0:1, :] = level
        column_labels[block, 1:2, :] = group
        lines += [level, group]
    lines.append(jnp.zeros((128 - 2 * SEEN, rows_dev), jnp.float32))
    row_labels[...] = jnp.transpose(jnp.concatenate(lines))


def labels_of(seen):
    rows_dev = seen.shape[2]
    return pl.pallas_call(
        labels_kernel,
        in_specs=[WHOLE],
        out_specs=[WHOLE] * 2,
        out_shape=[
            jax.ShapeDtypeStruct((rows_dev, 128), jnp.float32),
            jax.ShapeDtypeStruct((SEEN, 2, rows_dev), jnp.float32),
        ],
        compiler_params=params(),
        cost_estimate=SHORT,
        name="labels",
    )(seen)


def slot(block):
    other_plane = (block < 0) | (block >= OWN)
    return ((block + OWN) % GROUP) * 8 + jnp.where(other_plane, 2, 0)


def count_kernel(pairs, first, last, spot, *refs):
    held, (row_labels, column_labels, row_in, column_in), outs = refs[:4], refs[4:8], refs[8:]
    row_out, column_out = outs[-2:] if last else outs
    part = held[0].shape[1]
    half = column_labels.shape[2] // 2
    core, x, y = spot[0], spot[1], spot[2]
    here = pl.multiple_of(core * half, 128)
    there = pl.multiple_of((1 - core) * half, 128)
    if first:
        row_out[...] = jnp.zeros_like(row_out)
        column_out[...] = jnp.zeros_like(column_out)
    else:
        row_out[...] = row_in[...]
        column_out[...] = column_in[...]
    lanes = lax.broadcasted_iota(jnp.int32, (part, 128), 1)

    def tile(t, a, b):
        to_a, to_b = slot(a), slot(b)
        for at, side, one, two in ((0, here, x, y), (1, there, x if last else y, y if last else x)):
            rows = pl.ds(pl.multiple_of(((core * 2 + one) * 2 + two) * part, 8), part)
            columns = pl.ds(side, half)
            if last:
                share = pl.ds(at * half, half)
                score = added(held[0][t, :, share], held[1][t, :, share])
                score += added(held[2][t, :, share], held[3][t, :, share])
            else:
                score = added(held[2 * at][t], held[2 * at + 1][t])
            score = score.astype(jnp.float32) * (1.0 / SCALE)
            labels = row_labels[rows, :]
            lane = 2 * (a + BELOW)
            row_level = jnp.sum(jnp.where(lanes == lane, labels, 0.0), axis=1, keepdims=True)
            row_group = jnp.sum(jnp.where(lanes == lane + 1, labels, 0.0), axis=1, keepdims=True)
            column_level = column_labels[b + BELOW, 0:1, columns]
            column_group = column_labels[b + BELOW, 1:2, columns]
            same = row_group == column_group
            below = jnp.exp(score * (-1.0 / SOFTNESS_FACTOR))
            to_row = 1.0 / (1.0 + below * jnp.exp(row_level * (1.0 / SOFTNESS_FACTOR)))
            to_column = 1.0 / (1.0 + below * jnp.exp(column_level * (1.0 / SOFTNESS_FACTOR)))
            row_same = jnp.sum(jnp.where(same, to_row, 0.0), axis=1, keepdims=True)
            row_other = jnp.sum(jnp.where(same, 0.0, to_row), axis=1, keepdims=True)
            row_out[rows, :] += jnp.where(lanes == to_a, row_same, jnp.where(lanes == to_a + 1, row_other, 0.0))
            column_same = jnp.sum(jnp.where(same, to_column, 0.0), axis=0, keepdims=True)
            column_other = jnp.sum(jnp.where(same, 0.0, to_column), axis=0, keepdims=True)
            column_out[pl.ds(to_b, 1), columns] += column_same
            column_out[pl.ds(to_b + 1, 1), columns] += column_other

    loop(pairs, tile)
    if last:
        total = jnp.transpose(row_out[...])
        column_out[...] += total[: column_out.shape[0]]
        me = y * 2 + x
        for m in range(GROUP):
            outs[m][...] = column_out[pl.ds(pl.multiple_of((me ^ m) * 8, 8), 8), :]


def count(held, pairs, row_labels, column_labels, sums, last, spot):
    rows_dev = row_labels.shape[0]
    sum_shapes = [
        jax.ShapeDtypeStruct((rows_dev, 128), jnp.float32),
        jax.ShapeDtypeStruct((8 * GROUP, rows_dev), jnp.float32),
    ]
    out_shape = sum_shapes
    scratch = []
    if last:
        out_shape, scratch = [jax.ShapeDtypeStruct((8, rows_dev), jnp.float32)] * GROUP, [
            pltpu.VMEM(v.shape, v.dtype) for v in sum_shapes
        ]
    first = sums is None
    if first:
        sums = [jnp.zeros((8, 128), jnp.float32)] * 2
    return pl.pallas_call(
        functools.partial(count_kernel, pairs, first, last),
        in_specs=[SCALARS] + [WHOLE] * 8,
        out_specs=[WHOLE] * len(out_shape),
        out_shape=out_shape,
        scratch_shapes=scratch,
        compiler_params=params(),
        cost_estimate=SHORT,
        name="count",
    )(spot, *held, row_labels, column_labels, *sums)


def local(shape, features, group_index_list, threshold_codes):
    rows_dev, width = features.shape
    full = width * shape[1]
    half = rows_dev // 2
    quarter = width // GROUP
    chunks = tuple(n * quarter // 8 for n in SHARES)
    firsts = tuple(sum(chunks[:k]) for k in range(len(chunks)))
    row, core = lax.axis_index("rows"), lax.axis_index("feat")
    me = row % GROUP
    x, y = me % 2, me // 2
    spot = jnp.stack([core, x, y]).astype(jnp.int32)
    up, down = ring(shape, 1), ring(shape, -1)
    across = [(r * 2 + c, r * 2 + 1 - c) for r in range(shape[0]) for c in range(2)]

    given = [
        lax.dynamic_slice(features, ((1 - core) * half, q * quarter), (half, chunks[0])) for q in range(GROUP)
    ]
    soon = permute(jnp.concatenate(given, axis=1), across)
    widened = features.astype(jnp.float32)
    squares = lax.psum(jnp.sum(widened * widened, axis=1), "feat")
    got = permute(after(features, squares, soon), across)
    inverse = lax.rsqrt(squares / full + EPS) / math.sqrt(full)
    inverse = lax.dynamic_slice_in_dim(inverse, core * half, half, 0)[:, None]

    lanes = 2 * chunks[1]
    extra = -(-3 * rows_dev // (lanes * 16)) * 16
    labels = jnp.concatenate([group_index_list // DIGIT, group_index_list % DIGIT, threshold_codes])
    labels = jnp.pad(labels, (0, extra * lanes - 3 * rows_dev)).astype(jnp.bfloat16).reshape(extra, lanes)

    def part(mask, k):
        first = (me ^ mask) * quarter + firsts[k]
        cut = lax.dynamic_slice(features, (core * half, first), (half, chunks[k]))
        if k == 0:
            other = lax.dynamic_slice_in_dim(soon, (me ^ mask) * chunks[0], chunks[0], 1)
        else:
            other = lax.dynamic_slice(got, (core * half, first), (half, chunks[k]))
        cuts = (cut, other)
        cut = jnp.concatenate([(v.astype(jnp.float32) * inverse).astype(jnp.bfloat16) for v in cuts], axis=1)
        return jnp.concatenate([cut, labels]) if k == 1 else cut

    parts = [[part(m, k) for m in range(GROUP)] for k in range(len(chunks))]
    blocks, both, falling, from_below, from_above, got, earlier = [], [], [], [], [], [], []
    last = len(chunks) - 1
    near, far = (tuple((a + BELOW, b) for a, b in pairs) for pairs in (NEAR, FAR))
    plain = tuple((k, 0) for k in range(last))
    for k in range(len(chunks)):
        ready = [*got] if got else [None] * (GROUP - 1)
        got = [
            permute(after(parts[k][m], *ready[m - 1 : m][: k], *from_below[max(k - 2, 0) : max(k - 1, 0)]), swap(shape, m))
            for m in range(1, GROUP)
        ]
        waits = [p for later in parts[1:] for p in later] if k == 0 else [*earlier, both[-1]]
        if k == last:
            inner_sum = tiles_of(None, plain[:EARLIER], blocks[:EARLIER], both[:EARLIER], half, INNER, spot, final=False)
            waits.append(inner_sum)
        pieces = [after(v, *waits) for v in (parts[k][0], *got)]
        together, rising, sinking = arrange(pieces, me.reshape(1))
        blocks.append(together)
        falling.append(sinking)
        from_below.append(permute(after(rising, *earlier), up))
        both.append(permute(together, across))
        earlier = [from_below[-1]]
        if k in EARLY:
            from_above.append(permute(after(sinking[:, :half], both[k]), down))
            earlier.append(from_above[-1])
        if k == 1:
            labels_above = permute(after(sinking[:, half:], both[1]), down)
            earlier.append(labels_above)

    def reduce_x_y(tiles, *earlier):
        send_x, keep_x, send_y, keep_y = tiles
        got_x = permute(after(send_x, *earlier), swap(shape, 1))
        got_y = permute(after(send_y, *earlier), swap(shape, 2))
        return keep_x, got_x, keep_y, got_y

    def reduce_y_x(send_a, hold_a, send_b, hold_b):
        return hold_a, permute(send_a, swap(shape, 2)), hold_b, permute(send_b, swap(shape, 1))

    def tally(held, pairs, sums):
        return count(held, pairs, row_labels, column_labels, sums, pairs is UPPER, spot)

    upper = tuple((a - OWN, b) for a, b in UPPER)
    one = ((0, 0),)
    rest = tuple((k, 0) for k in range(len(chunks) - EARLIER))
    tiles = tiles_of(None, rest, blocks[EARLIER:], both[EARLIER:], half, INNER, spot, carry=inner_sum)
    inner = reduce_x_y(tiles)
    below = [after(v, tiles[0], tiles[2]) for v in from_below[:last]]
    plain = tuple((k, 0) for k in range(last))
    lower_sum = tiles_of(below, plain, blocks[:last], both[:last], half, near + far, spot, final=False)
    seen = jnp.concatenate([from_below[1][:, half:], blocks[1][:, half:], labels_above])
    seen = after(seen, *tiles).reshape(SEEN, -1)[:, : 3 * rows_dev].reshape(SEEN, 3, rows_dev)
    row_labels, column_labels = labels_of(seen)
    late = [k for k in range(len(chunks)) if k not in EARLY]
    falling = [after(v, lower_sum) for v in falling]
    falling = jnp.concatenate([falling[k][:, :half] for k in late], axis=2)
    from_above.append(permute(after(falling, lower_sum, column_labels, row_labels), down))

    one = ((0, 0),)
    ends = (blocks[last:], both[last:], half)
    near_below = [after(from_below[last], tiles[0], tiles[2])]
    tiles = tiles_of(near_below, one, *ends, near, spot, carry=lower_sum)
    near_held = reduce_x_y(tiles, inner[1], inner[3])
    far_below = [after(from_below[last], tiles[0], tiles[2])]
    far_held = reduce_x_y(tiles_of(far_below, one, *ends, far, spot, carry=lower_sum, skip=len(NEAR)), inner[1], inner[3])
    inner = reduce_y_x(*halve(*inner, spot))
    near_held = reduce_y_x(*halve(*near_held, spot))
    far_held = reduce_y_x(*halve(*far_held, spot))
    begins = {k: 2 * sum(chunks[i] for i in late if i < k) for k in late}
    starts = tuple((EARLY.index(k), 0) if k in EARLY else (len(EARLY), begins[k]) for k in range(len(chunks)))
    keep, *sends = tiles_of(from_above, starts, blocks, both, half, upper, spot, direct=True)
    upper_held = [keep] + [permute(v, swap(shape, m)) for m, v in enumerate(sends, 1)]
    sums = tally(inner, INNER, None)
    sums = tally(near_held, NEAR, sums)
    sums = tally(far_held, FAR, sums)
    sums = tally(upper_held, UPPER, sums)

    mine = sums[0]
    for m in range(1, GROUP):
        mine = mine + permute(sums[m], swap(shape, m))
    home = []
    for r in range(shape[0]):
        block = r % GROUP
        if block in (0, GROUP - 2, GROUP - 1):
            planes = 1 if block == 0 else -1
            home += [(r * 2 + c, (r + planes * GROUP) % shape[0] * 2 + c) for c in range(2)]
    mine = mine[:2] + permute(mine[2:4], home)
    return mine + permute(mine, across)


def solution(mesh):
    shape = (mesh.shape["rows"], mesh.shape["feat"])
    placed = (P("rows", "feat"), P("rows"), P("rows"))
    return jax.shard_map(
        functools.partial(local, shape), mesh=mesh, in_specs=placed, out_specs=P(None, "rows"), check_vma=False
    )
```

```python
import functools
import math

import jax
import jax.numpy as jnp
from jax import lax
from jax.experimental import pallas as pl
from jax.experimental.pallas import tpu as pltpu
from jax.sharding import PartitionSpec as P

MEET = 3
GROUP = MEET + 1
SOFTNESS_FACTOR = 0.02
EPS = 1e-06
SCALE = 32000.0
AXES = ("rows", "feat")
BELOW, OWN = 2, GROUP
SEEN = BELOW + OWN + 1
INNER = ((0, 1), (0, 2), (0, 3), (1, 3), (1, 2), (2, 3))
NEAR = ((-1, 0), (-1, 1), (-1, 2))
FAR = ((-2, 1), (-2, 0))
UPPER = ((4, 1),)
DIGIT = 64
SHARES = (2, 3, 3)
EARLY = (0,)
EARLIER = 2
CONTRACT = (((1,), (1,)), ((), ()))
SHORT = pl.CostEstimate(flops=1, bytes_accessed=1, transcendentals=0)


def params(mib=16):
    return pltpu.CompilerParams(vmem_limit_bytes=mib * 1024 * 1024)


def swap(count, mask):
    rows, cores = count
    return [(r * cores + c, (r ^ mask) * cores + c) for r in range(rows) for c in range(cores)]


def ring(count, planes):
    rows, cores = count
    return [(r * cores + c, (r + planes * GROUP) % rows * cores + c) for r in range(rows) for c in range(cores)]


def permute(value, pairs):
    return lax.ppermute(value, AXES, pairs)


def in_hbm(value):
    return pltpu.with_memory_space_constraint(value, pltpu.HBM)


def after(value, *earlier):
    return lax.optimization_barrier((value, *earlier))[0]


def to_fixed(value):
    return jnp.round(value * SCALE).astype(jnp.int32)


def added(one, two):
    return one.astype(jnp.int32) + two.astype(jnp.int32)


def tile_kernel(starts, count, carried, final, direct, table, *refs):
    own_refs, other_refs = refs[:count], refs[count : 2 * count]
    a_refs = refs[2 * count : (-5 if final else -1) - carried]
    total = refs[-1]
    half = total.shape[-2]
    rows = [a_refs[n][0, :half, first : first + ref.shape[2]] for (n, first), ref in zip(starts, own_refs)]
    rows = jnp.concatenate(rows, axis=1)
    own = [ref[0, :half, :] for ref in own_refs]
    other = [ref[0, :half, side] for ref in other_refs for side in halves(ref.shape[2])]
    columns = jnp.concatenate([jnp.concatenate(own, axis=1), jnp.concatenate(other, axis=1)])
    score = lax.dot_general(rows, columns, CONTRACT, preferred_element_type=jnp.float32)
    score = to_fixed(score)
    if carried:
        score = added(score, refs[-6 if final else -2][0])
    if not final:
        total[0] = score.astype(jnp.int16)
        return
    total[...] = score
    send_x, keep_x, send_y, keep_y = refs[-5:-1]
    part = half // 2
    at = 2 * pl.num_programs(0)
    x, y = table[at + 1], table[at + 2]
    if direct:
        part = part // 2
        for mask, out in enumerate(refs[-5:-1]):
            owner = (x ^ (mask & 1)) * 2 + (y ^ (mask >> 1))
            out[0] = total[pl.ds(pl.multiple_of(owner * part, 16), part), :].astype(jnp.int16)
        return
    for first, bit, send, keep in ((0, x, send_x, keep_x), (half, y, send_y, keep_y)):
        columns = pl.ds(first, half)
        send[0] = total[pl.ds(pl.multiple_of((1 - bit) * part, 16), part), columns].astype(jnp.int16)
        keep[0] = total[pl.ds(pl.multiple_of(bit * part, 16), part), columns].astype(jnp.int16)


def halves(width):
    return slice(width // 2, width), slice(0, width // 2)


def loop(pairs, body):
    if len(pairs) == 1:
        body(0, *pairs[0])
        return
    low = min(min(p) for p in pairs)
    codes = [sum((p[side] - low) << (3 * t) for t, p in enumerate(pairs)) for side in range(2)]

    def step(t, carry):
        a, b = (((jnp.int32(code) >> (3 * t)) & 7) + low for code in codes)
        body(t, a, b)
        return carry

    lax.fori_loop(0, len(pairs), step, 0)


SCALARS = pl.BlockSpec(memory_space=pltpu.SMEM)
WHOLE = pl.BlockSpec(memory_space=pltpu.VMEM)
ANYWHERE = pl.BlockSpec(memory_space=pl.ANY)


def tiles_of(a_arrays, starts, chunks, both, half, pairs, spot, carry=None, skip=0, final=True, direct=False):
    n = len(pairs)
    table = jnp.concatenate([jnp.array([a for a, _ in pairs] + [b for _, b in pairs], jnp.int32), spot])
    a_arrays = [in_hbm(v) for v in a_arrays] if a_arrays else chunks
    specs = [pl.BlockSpec((1, *v.shape[1:]), lambda t, s: (s[n + t], 0, 0)) for v in (*chunks, *both)]
    specs += [pl.BlockSpec((1, *v.shape[1:]), lambda t, s: (s[t], 0, 0)) for v in a_arrays]
    whole = pl.BlockSpec((1, half, 2 * half), lambda t, s: (t, 0, 0))
    depth = sum(v.shape[2] for v in chunks)
    carried = [] if carry is None else [carry]
    specs += [pl.BlockSpec((1, half, 2 * half), lambda t, s: (skip + t, 0, 0))] * len(carried)
    sent = pltpu.HBM((n, half // 2, half), jnp.int16)
    held = pltpu.HBM((n, half // 2, half), jnp.int16)
    out_specs = [pl.BlockSpec((1, half // 2, half), lambda t, s: (t, 0, 0))] * 4
    outs = [sent, held, sent, held]
    if direct:
        out_specs = [pl.BlockSpec((1, half // 4, 2 * half), lambda t, s: (t, 0, 0))] * 4
        held, sent = (f((n, half // 4, 2 * half), jnp.int16) for f in (jax.ShapeDtypeStruct, pltpu.HBM))
        outs = [held, sent, sent, sent]
    return pl.pallas_call(
        functools.partial(tile_kernel, starts, len(chunks), len(carried), final, direct),
        grid_spec=pltpu.PrefetchScalarGridSpec(
            num_scalar_prefetch=1,
            grid=(n,),
            in_specs=specs,
            out_specs=out_specs if final else whole,
            scratch_shapes=[pltpu.VMEM((half, 2 * half), jnp.int32)] if final else [],
        ),
        out_shape=outs if final else jax.ShapeDtypeStruct((n, half, 2 * half), jnp.int16),
        compiler_params=params(8 + depth // 192),
        cost_estimate=SHORT if final else pl.CostEstimate(flops=n * 4 * half * half * depth, bytes_accessed=n * 6 * half * depth, transcendentals=0),
        name="tiles",
    )(table, *chunks, *both, *a_arrays, *carried)


def arrange_kernel(me, *refs):
    pieces, together, rest = refs[:GROUP], refs[GROUP], refs[GROUP + 1 :]
    for m in range(GROUP):
        block = me[0] ^ m
        together[block] = pieces[m][...]

        if not rest:
            continue
        rising, falling = rest

        @pl.when(block >= GROUP - BELOW)
        def _():
            rising[block - (GROUP - BELOW)] = pieces[m][...]

        @pl.when(block == 0)
        def _():
            falling[0] = pieces[m][...]


def arrange(pieces, me, alone=False):
    rows, width = pieces[0].shape
    high, wide = (rows // 2, width) if rows % 32 == 0 else (rows, width // 2)

    def place(i):
        return (i, 0) if high < rows else (0, i)

    counts = (GROUP,) if alone else (GROUP, BELOW, 1)
    return pl.pallas_call(
        arrange_kernel,
        grid_spec=pltpu.PrefetchScalarGridSpec(
            num_scalar_prefetch=1,
            grid=(2,),
            in_specs=[pl.BlockSpec((high, wide), lambda i, s: place(i))] * GROUP,
            out_specs=[pl.BlockSpec((n, high, wide), lambda i, s: (0, *place(i))) for n in counts],
        ),
        out_shape=[jax.ShapeDtypeStruct((GROUP, rows, width), pieces[0].dtype)]
        + [pltpu.HBM((n, rows, width), pieces[0].dtype) for n in counts[1:]],
        compiler_params=params(),
        cost_estimate=SHORT,
        name="arrange",
    )(me, *pieces)


def halve_kernel(spot, keep_x, got_x, keep_y, got_y, send_a, hold_a, send_b, hold_b):
    part = send_a.shape[1]
    x, y = spot[1], spot[2]

    def step(t, carry):
        for keep, got, bit, send, hold in ((keep_x, got_x, y, send_a, hold_a), (keep_y, got_y, x, send_b, hold_b)):
            away = pl.ds(pl.multiple_of((1 - bit) * part, 16), part)
            here = pl.ds(pl.multiple_of(bit * part, 16), part)
            send[t] = added(keep[t, away, :], got[t, away, :]).astype(jnp.int16)
            hold[t] = added(keep[t, here, :], got[t, here, :]).astype(jnp.int16)
        return carry

    lax.fori_loop(0, send_a.shape[0], step, 0)


def halve(keep_x, got_x, keep_y, got_y, spot):
    n, rows, columns = keep_x.shape
    sent = held = jax.ShapeDtypeStruct((n, rows // 2, columns), jnp.int16)
    return pl.pallas_call(
        halve_kernel,
        in_specs=[SCALARS] + [WHOLE] * 4,
        out_specs=[WHOLE] * 4,
        out_shape=[sent, held, sent, held],
        compiler_params=params(),
        cost_estimate=SHORT,
        name="halve",
    )(spot, keep_x, got_x, keep_y, got_y)


def labels_kernel(seen, row_labels, column_labels):
    rows_dev = seen.shape[2]
    lines = []
    for block in range(SEEN):
        high, low, code = (seen[block, i : i + 1, :].astype(jnp.float32) for i in range(3))
        level, group = 0.2 + 0.15 * code, high * DIGIT + low
        column_labels[block, 0:1, :] = level
        column_labels[block, 1:2, :] = group
        lines += [level, group]
    lines.append(jnp.zeros((128 - 2 * SEEN, rows_dev), jnp.float32))
    row_labels[...] = jnp.transpose(jnp.concatenate(lines))


def labels_of(seen):
    rows_dev = seen.shape[2]
    return pl.pallas_call(
        labels_kernel,
        in_specs=[WHOLE],
        out_specs=[WHOLE] * 2,
        out_shape=[
            jax.ShapeDtypeStruct((rows_dev, 128), jnp.float32),
            jax.ShapeDtypeStruct((SEEN, 2, rows_dev), jnp.float32),
        ],
        compiler_params=params(),
        cost_estimate=SHORT,
        name="labels",
    )(seen)


def slot(block):
    other_plane = (block < 0) | (block >= OWN)
    return ((block + OWN) % GROUP) * 8 + jnp.where(other_plane, 2, 0)


def count_kernel(pairs, first, last, spot, *refs):
    held, (row_labels, column_labels, row_in, column_in), outs = refs[:4], refs[4:8], refs[8:]
    row_out, column_out = outs[-2:] if last else outs
    part = held[0].shape[1]
    half = column_labels.shape[2] // 2
    core, x, y = spot[0], spot[1], spot[2]
    here = pl.multiple_of(core * half, 128)
    there = pl.multiple_of((1 - core) * half, 128)
    if first:
        row_out[...] = jnp.zeros_like(row_out)
        column_out[...] = jnp.zeros_like(column_out)
    else:
        row_out[...] = row_in[...]
        column_out[...] = column_in[...]
    lanes = lax.broadcasted_iota(jnp.int32, (part, 128), 1)

    def tile(t, a, b):
        to_a, to_b = slot(a), slot(b)
        for at, side, one, two in ((0, here, x, y), (1, there, x if last else y, y if last else x)):
            rows = pl.ds(pl.multiple_of(((core * 2 + one) * 2 + two) * part, 8), part)
            columns = pl.ds(side, half)
            if last:
                share = pl.ds(at * half, half)
                score = added(held[0][t, :, share], held[1][t, :, share])
                score += added(held[2][t, :, share], held[3][t, :, share])
            else:
                score = added(held[2 * at][t], held[2 * at + 1][t])
            score = score.astype(jnp.float32) * (1.0 / SCALE)
            labels = row_labels[rows, :]
            lane = 2 * (a + BELOW)
            row_level = jnp.sum(jnp.where(lanes == lane, labels, 0.0), axis=1, keepdims=True)
            row_group = jnp.sum(jnp.where(lanes == lane + 1, labels, 0.0), axis=1, keepdims=True)
            column_level = column_labels[b + BELOW, 0:1, columns]
            column_group = column_labels[b + BELOW, 1:2, columns]
            same = row_group == column_group
            below = jnp.exp(score * (-1.0 / SOFTNESS_FACTOR))
            to_row = 1.0 / (1.0 + below * jnp.exp(row_level * (1.0 / SOFTNESS_FACTOR)))
            to_column = 1.0 / (1.0 + below * jnp.exp(column_level * (1.0 / SOFTNESS_FACTOR)))
            row_same = jnp.sum(jnp.where(same, to_row, 0.0), axis=1, keepdims=True)
            row_other = jnp.sum(jnp.where(same, 0.0, to_row), axis=1, keepdims=True)
            row_out[rows, :] += jnp.where(lanes == to_a, row_same, jnp.where(lanes == to_a + 1, row_other, 0.0))
            column_same = jnp.sum(jnp.where(same, to_column, 0.0), axis=0, keepdims=True)
            column_other = jnp.sum(jnp.where(same, 0.0, to_column), axis=0, keepdims=True)
            column_out[pl.ds(to_b, 1), columns] += column_same
            column_out[pl.ds(to_b + 1, 1), columns] += column_other

    loop(pairs, tile)
    if last:
        total = jnp.transpose(row_out[...])
        column_out[...] += total[: column_out.shape[0]]
        me = y * 2 + x
        for m in range(GROUP):
            outs[m][...] = column_out[pl.ds(pl.multiple_of((me ^ m) * 8, 8), 8), :]


def count(held, pairs, row_labels, column_labels, sums, last, spot):
    rows_dev = row_labels.shape[0]
    sum_shapes = [
        jax.ShapeDtypeStruct((rows_dev, 128), jnp.float32),
        jax.ShapeDtypeStruct((8 * GROUP, rows_dev), jnp.float32),
    ]
    out_shape = sum_shapes
    scratch = []
    if last:
        out_shape, scratch = [jax.ShapeDtypeStruct((8, rows_dev), jnp.float32)] * GROUP, [
            pltpu.VMEM(v.shape, v.dtype) for v in sum_shapes
        ]
    first = sums is None
    if first:
        sums = [jnp.zeros((8, 128), jnp.float32)] * 2
    return pl.pallas_call(
        functools.partial(count_kernel, pairs, first, last),
        in_specs=[SCALARS] + [WHOLE] * 8,
        out_specs=[WHOLE] * len(out_shape),
        out_shape=out_shape,
        scratch_shapes=scratch,
        compiler_params=params(),
        cost_estimate=SHORT,
        name="count",
    )(spot, *held, row_labels, column_labels, *sums)


def local(shape, features, group_index_list, threshold_codes):
    rows_dev, width = features.shape
    full = width * shape[1]
    half = rows_dev // 2
    quarter = width // GROUP
    chunks = tuple(n * quarter // 8 for n in SHARES)
    firsts = tuple(sum(chunks[:k]) for k in range(len(chunks)))
    row, core = lax.axis_index("rows"), lax.axis_index("feat")
    me = row % GROUP
    x, y = me % 2, me // 2
    spot = jnp.stack([core, x, y]).astype(jnp.int32)
    up, down = ring(shape, 1), ring(shape, -1)
    across = [(r * 2 + c, r * 2 + 1 - c) for r in range(shape[0]) for c in range(2)]

    given = [
        lax.dynamic_slice(features, ((1 - core) * half, q * quarter), (half, chunks[0])) for q in range(GROUP)
    ]
    soon = permute(jnp.concatenate(given, axis=1), across)
    widened = features.astype(jnp.float32)
    squares = lax.psum(jnp.sum(widened * widened, axis=1), "feat")
    got = permute(after(features, squares, soon), across)
    inverse = lax.rsqrt(squares / full + EPS) / math.sqrt(full)
    inverse = lax.dynamic_slice_in_dim(inverse, core * half, half, 0)[:, None]

    lanes = 2 * chunks[1]
    extra = -(-3 * rows_dev // (lanes * 16)) * 16
    labels = jnp.concatenate([group_index_list // DIGIT, group_index_list % DIGIT, threshold_codes])
    labels = jnp.pad(labels, (0, extra * lanes - 3 * rows_dev)).astype(jnp.bfloat16).reshape(extra, lanes)

    def part(mask, k):
        first = (me ^ mask) * quarter + firsts[k]
        cut = lax.dynamic_slice(features, (core * half, first), (half, chunks[k]))
        if k == 0:
            other = lax.dynamic_slice_in_dim(soon, (me ^ mask) * chunks[0], chunks[0], 1)
        else:
            other = lax.dynamic_slice(got, (core * half, first), (half, chunks[k]))
        cuts = (cut, other)
        cut = jnp.concatenate([(v.astype(jnp.float32) * inverse).astype(jnp.bfloat16) for v in cuts], axis=1)
        return jnp.concatenate([cut, labels]) if k == 1 else cut

    parts = [[part(m, k) for m in range(GROUP)] for k in range(len(chunks))]
    blocks, both, falling, from_below, from_above, got, earlier = [], [], [], [], [], [], []
    last = len(chunks) - 1
    near, far = (tuple((a + BELOW, b) for a, b in pairs) for pairs in (NEAR, FAR))
    plain = tuple((k, 0) for k in range(last))
    for k in range(len(chunks)):
        ready = [*got] if got else [None] * (GROUP - 1)
        got = [
            permute(after(parts[k][m], *ready[m - 1 : m][: k], *from_below[max(k - 2, 0) : max(k - 1, 0)]), swap(shape, m))
            for m in range(1, GROUP)
        ]
        waits = [p for later in parts[1:] for p in later] if k == 0 else [*earlier, both[-1]]
        if k == last:
            inner_sum = tiles_of(None, plain[:EARLIER], blocks[:EARLIER], both[:EARLIER], half, INNER, spot, final=False)
            waits.append(inner_sum)
        pieces = [after(v, *waits) for v in (parts[k][0], *got)]
        together, *others = arrange(pieces, me.reshape(1), k == last)
        rising, sinking = others or (together[GROUP - BELOW :], together[:1])
        blocks.append(together)
        falling.append(sinking)
        from_below.append(permute(after(rising, *earlier), up))
        both.append(permute(together, across))
        earlier = [from_below[-1]]
        if k in EARLY:
            from_above.append(permute(after(sinking[:, :half], both[k]), down))
            earlier.append(from_above[-1])
        if k == 1:
            labels_above = permute(after(sinking[:, half:], both[1]), down)
            earlier.append(labels_above)

    def reduce_x_y(tiles, *earlier):
        send_x, keep_x, send_y, keep_y = tiles
        got_x = permute(after(send_x, *earlier), swap(shape, 1))
        got_y = permute(after(send_y, *earlier), swap(shape, 2))
        return keep_x, got_x, keep_y, got_y

    def reduce_y_x(send_a, hold_a, send_b, hold_b):
        return hold_a, permute(send_a, swap(shape, 2)), hold_b, permute(send_b, swap(shape, 1))

    def tally(held, pairs, sums):
        return count(held, pairs, row_labels, column_labels, sums, pairs is UPPER, spot)

    upper = tuple((a - OWN, b) for a, b in UPPER)
    one = ((0, 0),)
    rest = tuple((k, 0) for k in range(len(chunks) - EARLIER))
    tiles = tiles_of(None, rest, blocks[EARLIER:], both[EARLIER:], half, INNER, spot, carry=inner_sum)
    inner = reduce_x_y(tiles)
    below = [after(v, tiles[0], tiles[2]) for v in from_below[:last]]
    plain = tuple((k, 0) for k in range(last))
    lower_sum = tiles_of(below, plain, blocks[:last], both[:last], half, near + far, spot, final=False)
    seen = jnp.concatenate([from_below[1][:, half:], blocks[1][:, half:], labels_above])
    seen = after(seen, *tiles).reshape(SEEN, -1)[:, : 3 * rows_dev].reshape(SEEN, 3, rows_dev)
    row_labels, column_labels = labels_of(seen)
    late = [k for k in range(len(chunks)) if k not in EARLY]
    falling = [after(v, lower_sum) for v in falling]
    falling = jnp.concatenate([falling[k][:, :half] for k in late], axis=2)
    from_above.append(permute(after(falling, lower_sum, column_labels, row_labels), down))

    one = ((0, 0),)
    ends = (blocks[last:], both[last:], half)
    near_below = [after(from_below[last], tiles[0], tiles[2])]
    tiles = tiles_of(near_below, one, *ends, near, spot, carry=lower_sum)
    near_held = reduce_x_y(tiles, inner[1], inner[3])
    far_below = [after(from_below[last], tiles[0], tiles[2])]
    far_held = reduce_x_y(tiles_of(far_below, one, *ends, far, spot, carry=lower_sum, skip=len(NEAR)), inner[1], inner[3])
    inner = reduce_y_x(*halve(*inner, spot))
    near_held = reduce_y_x(*halve(*near_held, spot))
    far_held = reduce_y_x(*halve(*far_held, spot))
    begins = {k: 2 * sum(chunks[i] for i in late if i < k) for k in late}
    starts = tuple((EARLY.index(k), 0) if k in EARLY else (len(EARLY), begins[k]) for k in range(len(chunks)))
    keep, *sends = tiles_of(from_above, starts, blocks, both, half, upper, spot, direct=True)
    upper_held = [keep] + [permute(v, swap(shape, m)) for m, v in enumerate(sends, 1)]
    sums = tally(inner, INNER, None)
    sums = tally(near_held, NEAR, sums)
    sums = tally(far_held, FAR, sums)
    sums = tally(upper_held, UPPER, sums)

    mine = sums[0]
    for m in range(1, GROUP):
        mine = mine + permute(sums[m], swap(shape, m))
    home = []
    for r in range(shape[0]):
        block = r % GROUP
        if block in (0, GROUP - 2, GROUP - 1):
            planes = 1 if block == 0 else -1
            home += [(r * 2 + c, (r + planes * GROUP) % shape[0] * 2 + c) for c in range(2)]
    mine = mine[:2] + permute(mine[2:4], home)
    return mine + permute(mine, across)


def solution(mesh):
    shape = (mesh.shape["rows"], mesh.shape["feat"])
    placed = (P("rows", "feat"), P("rows"), P("rows"))
    return jax.shard_map(
        functools.partial(local, shape), mesh=mesh, in_specs=placed, out_specs=P(None, "rows"), check_vma=False
    )
```

```python
import functools
import math

import jax
import jax.numpy as jnp
from jax import lax
from jax.experimental import pallas as pl
from jax.experimental.pallas import tpu as pltpu
from jax.sharding import PartitionSpec as P

MEET = 3
GROUP = MEET + 1
SOFTNESS_FACTOR = 0.02
EPS = 1e-06
SCALE = 32000.0
AXES = ("rows", "feat")
BELOW, OWN = 2, GROUP
SEEN = BELOW + OWN + 1
INNER = ((0, 1), (0, 2), (0, 3), (1, 3), (1, 2), (2, 3))
NEAR = ((-1, 0), (-1, 1), (-1, 2))
FAR = ((-2, 1), (-2, 0))
UPPER = ((4, 1),)
DIGIT = 64
SHARES = (2, 3, 3)
EARLY = (0,)
EARLIER = 2
CONTRACT = (((1,), (1,)), ((), ()))
SHORT = pl.CostEstimate(flops=1, bytes_accessed=1, transcendentals=0)


def params(mib=16):
    return pltpu.CompilerParams(vmem_limit_bytes=mib * 1024 * 1024)


def swap(count, mask):
    rows, cores = count
    return [(r * cores + c, (r ^ mask) * cores + c) for r in range(rows) for c in range(cores)]


def ring(count, planes):
    rows, cores = count
    return [(r * cores + c, (r + planes * GROUP) % rows * cores + c) for r in range(rows) for c in range(cores)]


def permute(value, pairs):
    return lax.ppermute(value, AXES, pairs)


def in_hbm(value):
    return pltpu.with_memory_space_constraint(value, pltpu.HBM)


def after(value, *earlier):
    return lax.optimization_barrier((value, *earlier))[0]


def to_fixed(value):
    return jnp.round(value * SCALE).astype(jnp.int32)


def added(one, two):
    return one.astype(jnp.int32) + two.astype(jnp.int32)


def tile_kernel(starts, count, carried, final, direct, table, *refs):
    own_refs, other_refs = refs[:count], refs[count : 2 * count]
    a_refs = refs[2 * count : (-5 if final else -1) - carried]
    total = refs[-1]
    half = total.shape[-2]
    rows = [a_refs[n][0, :half, first : first + ref.shape[2]] for (n, first), ref in zip(starts, own_refs)]
    rows = jnp.concatenate(rows, axis=1)
    own = [ref[0, :half, :] for ref in own_refs]
    other = [ref[0, :half, side] for ref in other_refs for side in halves(ref.shape[2])]
    columns = jnp.concatenate([jnp.concatenate(own, axis=1), jnp.concatenate(other, axis=1)])
    score = lax.dot_general(rows, columns, CONTRACT, preferred_element_type=jnp.float32)
    score = to_fixed(score)
    if carried:
        score = added(score, refs[-6 if final else -2][0])
    if not final:
        total[0] = score.astype(jnp.int16)
        return
    total[...] = score
    send_x, keep_x, send_y, keep_y = refs[-5:-1]
    part = half // 2
    at = 2 * pl.num_programs(0)
    x, y = table[at + 1], table[at + 2]
    if direct:
        part = part // 2
        for mask, out in enumerate(refs[-5:-1]):
            owner = (x ^ (mask & 1)) * 2 + (y ^ (mask >> 1))
            out[0] = total[pl.ds(pl.multiple_of(owner * part, 16), part), :].astype(jnp.int16)
        return
    for first, bit, send, keep in ((0, x, send_x, keep_x), (half, y, send_y, keep_y)):
        columns = pl.ds(first, half)
        send[0] = total[pl.ds(pl.multiple_of((1 - bit) * part, 16), part), columns].astype(jnp.int16)
        keep[0] = total[pl.ds(pl.multiple_of(bit * part, 16), part), columns].astype(jnp.int16)


def halves(width):
    return slice(width // 2, width), slice(0, width // 2)


def loop(pairs, body):
    if len(pairs) == 1:
        body(0, *pairs[0])
        return
    low = min(min(p) for p in pairs)
    codes = [sum((p[side] - low) << (3 * t) for t, p in enumerate(pairs)) for side in range(2)]

    def step(t, carry):
        a, b = (((jnp.int32(code) >> (3 * t)) & 7) + low for code in codes)
        body(t, a, b)
        return carry

    lax.fori_loop(0, len(pairs), step, 0)


SCALARS = pl.BlockSpec(memory_space=pltpu.SMEM)
WHOLE = pl.BlockSpec(memory_space=pltpu.VMEM)
ANYWHERE = pl.BlockSpec(memory_space=pl.ANY)


def tiles_of(a_arrays, starts, chunks, both, half, pairs, spot, carry=None, skip=0, final=True, direct=False):
    n = len(pairs)
    table = jnp.concatenate([jnp.array([a for a, _ in pairs] + [b for _, b in pairs], jnp.int32), spot])
    a_arrays = [in_hbm(v) for v in a_arrays] if a_arrays else chunks
    specs = [pl.BlockSpec((1, *v.shape[1:]), lambda t, s: (s[n + t], 0, 0)) for v in (*chunks, *both)]
    specs += [pl.BlockSpec((1, *v.shape[1:]), lambda t, s: (s[t], 0, 0)) for v in a_arrays]
    whole = pl.BlockSpec((1, half, 2 * half), lambda t, s: (t, 0, 0))
    depth = sum(v.shape[2] for v in chunks)
    carried = [] if carry is None else [carry]
    specs += [pl.BlockSpec((1, half, 2 * half), lambda t, s: (skip + t, 0, 0))] * len(carried)
    sent = pltpu.HBM((n, half // 2, half), jnp.int16)
    held = pltpu.HBM((n, half // 2, half), jnp.int16)
    out_specs = [pl.BlockSpec((1, half // 2, half), lambda t, s: (t, 0, 0))] * 4
    outs = [sent, held, sent, held]
    if direct:
        out_specs = [pl.BlockSpec((1, half // 4, 2 * half), lambda t, s: (t, 0, 0))] * 4
        held, sent = (f((n, half // 4, 2 * half), jnp.int16) for f in (jax.ShapeDtypeStruct, pltpu.HBM))
        outs = [held, sent, sent, sent]
    return pl.pallas_call(
        functools.partial(tile_kernel, starts, len(chunks), len(carried), final, direct),
        grid_spec=pltpu.PrefetchScalarGridSpec(
            num_scalar_prefetch=1,
            grid=(n,),
            in_specs=specs,
            out_specs=out_specs if final else whole,
            scratch_shapes=[pltpu.VMEM((half, 2 * half), jnp.int32)] if final else [],
        ),
        out_shape=outs if final else jax.ShapeDtypeStruct((n, half, 2 * half), jnp.int16),
        compiler_params=params(8 + depth // 192),
        cost_estimate=SHORT if final else pl.CostEstimate(flops=n * 4 * half * half * depth, bytes_accessed=n * 6 * half * depth, transcendentals=0),
        name="tiles",
    )(table, *chunks, *both, *a_arrays, *carried)


def squares_kernel(*refs):
    out = refs[-1]
    total = jnp.zeros((out.shape[1], 128), jnp.float32)
    for ref in refs[:-1]:
        for first in range(0, ref.shape[1], 128):
            value = ref[:, first : first + 128].astype(jnp.float32)
            total += value * value
    out[...] = jnp.sum(jnp.transpose(total), axis=0, keepdims=True)


def squares_of(features):
    rows, width = features.shape
    step = 384 if rows % 384 == 0 else rows
    windows = GROUP
    return pl.pallas_call(
        squares_kernel,
        grid=(rows // step,),
        in_specs=[
            pl.BlockSpec((step, width // windows), functools.partial(lambda at, i: (i, at), at)) for at in range(windows)
        ],
        out_specs=pl.BlockSpec((1, step), lambda i: (0, i)),
        out_shape=jax.ShapeDtypeStruct((1, rows), jnp.float32),
        compiler_params=params(),
        cost_estimate=SHORT,
        name="squares",
    )(*[in_hbm(features)] * windows)[0]


def arrange_kernel(me, *refs):
    pieces, together, rest = refs[:GROUP], refs[GROUP], refs[GROUP + 1 :]
    for m in range(GROUP):
        block = me[0] ^ m
        together[block] = pieces[m][...]

        if not rest:
            continue
        rising, falling = rest

        @pl.when(block >= GROUP - BELOW)
        def _():
            rising[block - (GROUP - BELOW)] = pieces[m][...]

        @pl.when(block == 0)
        def _():
            falling[0] = pieces[m][...]


def arrange(pieces, me, alone=False):
    rows, width = pieces[0].shape
    high, wide = (rows // 2, width) if rows % 32 == 0 else (rows, width // 2)

    def place(i):
        return (i, 0) if high < rows else (0, i)

    counts = (GROUP,) if alone else (GROUP, BELOW, 1)
    return pl.pallas_call(
        arrange_kernel,
        grid_spec=pltpu.PrefetchScalarGridSpec(
            num_scalar_prefetch=1,
            grid=(2,),
            in_specs=[pl.BlockSpec((high, wide), lambda i, s: place(i))] * GROUP,
            out_specs=[pl.BlockSpec((n, high, wide), lambda i, s: (0, *place(i))) for n in counts],
        ),
        out_shape=[jax.ShapeDtypeStruct((GROUP, rows, width), pieces[0].dtype)]
        + [pltpu.HBM((n, rows, width), pieces[0].dtype) for n in counts[1:]],
        compiler_params=params(),
        cost_estimate=SHORT,
        name="arrange",
    )(me, *pieces)


def halve_kernel(spot, keep_x, got_x, keep_y, got_y, send_a, hold_a, send_b, hold_b):
    part = send_a.shape[1]
    x, y = spot[1], spot[2]

    def step(t, carry):
        for keep, got, bit, send, hold in ((keep_x, got_x, y, send_a, hold_a), (keep_y, got_y, x, send_b, hold_b)):
            away = pl.ds(pl.multiple_of((1 - bit) * part, 16), part)
            here = pl.ds(pl.multiple_of(bit * part, 16), part)
            send[t] = added(keep[t, away, :], got[t, away, :]).astype(jnp.int16)
            hold[t] = added(keep[t, here, :], got[t, here, :]).astype(jnp.int16)
        return carry

    lax.fori_loop(0, send_a.shape[0], step, 0)


def halve(keep_x, got_x, keep_y, got_y, spot):
    n, rows, columns = keep_x.shape
    sent = held = jax.ShapeDtypeStruct((n, rows // 2, columns), jnp.int16)
    return pl.pallas_call(
        halve_kernel,
        in_specs=[SCALARS] + [WHOLE] * 4,
        out_specs=[WHOLE] * 4,
        out_shape=[sent, held, sent, held],
        compiler_params=params(),
        cost_estimate=SHORT,
        name="halve",
    )(spot, keep_x, got_x, keep_y, got_y)


def labels_kernel(seen, row_labels, column_labels):
    rows_dev = seen.shape[2]
    lines = []
    for block in range(SEEN):
        high, low, code = (seen[block, i : i + 1, :].astype(jnp.float32) for i in range(3))
        level, group = 0.2 + 0.15 * code, high * DIGIT + low
        column_labels[block, 0:1, :] = level
        column_labels[block, 1:2, :] = group
        lines += [level, group]
    lines.append(jnp.zeros((128 - 2 * SEEN, rows_dev), jnp.float32))
    row_labels[...] = jnp.transpose(jnp.concatenate(lines))


def labels_of(seen):
    rows_dev = seen.shape[2]
    return pl.pallas_call(
        labels_kernel,
        in_specs=[WHOLE],
        out_specs=[WHOLE] * 2,
        out_shape=[
            jax.ShapeDtypeStruct((rows_dev, 128), jnp.float32),
            jax.ShapeDtypeStruct((SEEN, 2, rows_dev), jnp.float32),
        ],
        compiler_params=params(),
        cost_estimate=SHORT,
        name="labels",
    )(seen)


def slot(block):
    other_plane = (block < 0) | (block >= OWN)
    return ((block + OWN) % GROUP) * 8 + jnp.where(other_plane, 2, 0)


def count_kernel(pairs, first, last, spot, *refs):
    held, (row_labels, column_labels, row_in, column_in), outs = refs[:4], refs[4:8], refs[8:]
    row_out, column_out = outs[-2:] if last else outs
    part = held[0].shape[1]
    half = column_labels.shape[2] // 2
    core, x, y = spot[0], spot[1], spot[2]
    here = pl.multiple_of(core * half, 128)
    there = pl.multiple_of((1 - core) * half, 128)
    if first:
        row_out[...] = jnp.zeros_like(row_out)
        column_out[...] = jnp.zeros_like(column_out)
    else:
        row_out[...] = row_in[...]
        column_out[...] = column_in[...]
    lanes = lax.broadcasted_iota(jnp.int32, (part, 128), 1)

    def tile(t, a, b):
        to_a, to_b = slot(a), slot(b)
        for at, side, one, two in ((0, here, x, y), (1, there, x if last else y, y if last else x)):
            rows = pl.ds(pl.multiple_of(((core * 2 + one) * 2 + two) * part, 8), part)
            columns = pl.ds(side, half)
            if last:
                share = pl.ds(at * half, half)
                score = added(held[0][t, :, share], held[1][t, :, share])
                score += added(held[2][t, :, share], held[3][t, :, share])
            else:
                score = added(held[2 * at][t], held[2 * at + 1][t])
            score = score.astype(jnp.float32) * (1.0 / SCALE)
            labels = row_labels[rows, :]
            lane = 2 * (a + BELOW)
            row_level = jnp.sum(jnp.where(lanes == lane, labels, 0.0), axis=1, keepdims=True)
            row_group = jnp.sum(jnp.where(lanes == lane + 1, labels, 0.0), axis=1, keepdims=True)
            column_level = column_labels[b + BELOW, 0:1, columns]
            column_group = column_labels[b + BELOW, 1:2, columns]
            same = row_group == column_group
            below = jnp.exp(score * (-1.0 / SOFTNESS_FACTOR))
            to_row = 1.0 / (1.0 + below * jnp.exp(row_level * (1.0 / SOFTNESS_FACTOR)))
            to_column = 1.0 / (1.0 + below * jnp.exp(column_level * (1.0 / SOFTNESS_FACTOR)))
            row_same = jnp.sum(jnp.where(same, to_row, 0.0), axis=1, keepdims=True)
            row_other = jnp.sum(jnp.where(same, 0.0, to_row), axis=1, keepdims=True)
            row_out[rows, :] += jnp.where(lanes == to_a, row_same, jnp.where(lanes == to_a + 1, row_other, 0.0))
            column_same = jnp.sum(jnp.where(same, to_column, 0.0), axis=0, keepdims=True)
            column_other = jnp.sum(jnp.where(same, 0.0, to_column), axis=0, keepdims=True)
            column_out[pl.ds(to_b, 1), columns] += column_same
            column_out[pl.ds(to_b + 1, 1), columns] += column_other

    loop(pairs, tile)
    if last:
        total = jnp.transpose(row_out[...])
        column_out[...] += total[: column_out.shape[0]]
        me = y * 2 + x
        for m in range(GROUP):
            outs[m][...] = column_out[pl.ds(pl.multiple_of((me ^ m) * 8, 8), 8), :]


def count(held, pairs, row_labels, column_labels, sums, last, spot):
    rows_dev = row_labels.shape[0]
    sum_shapes = [
        jax.ShapeDtypeStruct((rows_dev, 128), jnp.float32),
        jax.ShapeDtypeStruct((8 * GROUP, rows_dev), jnp.float32),
    ]
    out_shape = sum_shapes
    scratch = []
    if last:
        out_shape, scratch = [jax.ShapeDtypeStruct((8, rows_dev), jnp.float32)] * GROUP, [
            pltpu.VMEM(v.shape, v.dtype) for v in sum_shapes
        ]
    first = sums is None
    if first:
        sums = [jnp.zeros((8, 128), jnp.float32)] * 2
    return pl.pallas_call(
        functools.partial(count_kernel, pairs, first, last),
        in_specs=[SCALARS] + [WHOLE] * 8,
        out_specs=[WHOLE] * len(out_shape),
        out_shape=out_shape,
        scratch_shapes=scratch,
        compiler_params=params(),
        cost_estimate=SHORT,
        name="count",
    )(spot, *held, row_labels, column_labels, *sums)


def local(shape, features, group_index_list, threshold_codes):
    rows_dev, width = features.shape
    full = width * shape[1]
    half = rows_dev // 2
    quarter = width // GROUP
    chunks = tuple(n * quarter // 8 for n in SHARES)
    firsts = tuple(sum(chunks[:k]) for k in range(len(chunks)))
    row, core = lax.axis_index("rows"), lax.axis_index("feat")
    me = row % GROUP
    x, y = me % 2, me // 2
    spot = jnp.stack([core, x, y]).astype(jnp.int32)
    up, down = ring(shape, 1), ring(shape, -1)
    across = [(r * 2 + c, r * 2 + 1 - c) for r in range(shape[0]) for c in range(2)]

    given = [
        lax.dynamic_slice(features, ((1 - core) * half, q * quarter), (half, chunks[0])) for q in range(GROUP)
    ]
    soon = permute(jnp.concatenate(given, axis=1), across)
    squares = lax.psum(squares_of(features), "feat")
    got = permute(after(features, squares, soon), across)
    inverse = lax.rsqrt(squares / full + EPS) / math.sqrt(full)
    inverse = lax.dynamic_slice_in_dim(inverse, core * half, half, 0)[:, None]

    lanes = 2 * chunks[1]
    extra = -(-3 * rows_dev // (lanes * 16)) * 16
    labels = jnp.concatenate([group_index_list // DIGIT, group_index_list % DIGIT, threshold_codes])
    labels = jnp.pad(labels, (0, extra * lanes - 3 * rows_dev)).astype(jnp.bfloat16).reshape(extra, lanes)

    def part(mask, k):
        first = (me ^ mask) * quarter + firsts[k]
        cut = lax.dynamic_slice(features, (core * half, first), (half, chunks[k]))
        if k == 0:
            other = lax.dynamic_slice_in_dim(soon, (me ^ mask) * chunks[0], chunks[0], 1)
        else:
            other = lax.dynamic_slice(got, (core * half, first), (half, chunks[k]))
        cuts = (cut, other)
        cut = jnp.concatenate([(v.astype(jnp.float32) * inverse).astype(jnp.bfloat16) for v in cuts], axis=1)
        return jnp.concatenate([cut, labels]) if k == 1 else cut

    parts = [[part(m, k) for m in range(GROUP)] for k in range(len(chunks))]
    blocks, both, falling, from_below, from_above, got, earlier = [], [], [], [], [], [], []
    last = len(chunks) - 1
    near, far = (tuple((a + BELOW, b) for a, b in pairs) for pairs in (NEAR, FAR))
    plain = tuple((k, 0) for k in range(last))
    for k in range(len(chunks)):
        ready = [*got] if got else [None] * (GROUP - 1)
        got = [
            permute(after(parts[k][m], *ready[m - 1 : m][: k], *from_below[max(k - 2, 0) : max(k - 1, 0)]), swap(shape, m))
            for m in range(1, GROUP)
        ]
        waits = [p for later in parts[1:] for p in later] if k == 0 else [*earlier, both[-1]]
        if k == last:
            inner_sum = tiles_of(None, plain[:EARLIER], blocks[:EARLIER], both[:EARLIER], half, INNER, spot, final=False)
            waits.append(inner_sum)
        pieces = [after(v, *waits) for v in (parts[k][0], *got)]
        together, *others = arrange(pieces, me.reshape(1), k == last)
        rising, sinking = others or (together[GROUP - BELOW :], together[:1])
        blocks.append(together)
        falling.append(sinking)
        from_below.append(permute(after(rising, *earlier), up))
        both.append(permute(together, across))
        earlier = [from_below[-1]]
        if k in EARLY:
            from_above.append(permute(after(sinking[:, :half], both[k]), down))
            earlier.append(from_above[-1])
        if k == 1:
            labels_above = permute(after(sinking[:, half:], both[1]), down)
            earlier.append(labels_above)

    def reduce_x_y(tiles, *earlier):
        send_x, keep_x, send_y, keep_y = tiles
        got_x = permute(after(send_x, *earlier), swap(shape, 1))
        got_y = permute(after(send_y, *earlier), swap(shape, 2))
        return keep_x, got_x, keep_y, got_y

    def reduce_y_x(send_a, hold_a, send_b, hold_b):
        return hold_a, permute(send_a, swap(shape, 2)), hold_b, permute(send_b, swap(shape, 1))

    def tally(held, pairs, sums):
        return count(held, pairs, row_labels, column_labels, sums, pairs is UPPER, spot)

    upper = tuple((a - OWN, b) for a, b in UPPER)
    one = ((0, 0),)
    rest = tuple((k, 0) for k in range(len(chunks) - EARLIER))
    tiles = tiles_of(None, rest, blocks[EARLIER:], both[EARLIER:], half, INNER, spot, carry=inner_sum)
    inner = reduce_x_y(tiles)
    below = [after(v, tiles[0], tiles[2]) for v in from_below[:last]]
    plain = tuple((k, 0) for k in range(last))
    lower_sum = tiles_of(below, plain, blocks[:last], both[:last], half, near + far, spot, final=False)
    seen = jnp.concatenate([from_below[1][:, half:], blocks[1][:, half:], labels_above])
    seen = after(seen, *tiles).reshape(SEEN, -1)[:, : 3 * rows_dev].reshape(SEEN, 3, rows_dev)
    row_labels, column_labels = labels_of(seen)
    late = [k for k in range(len(chunks)) if k not in EARLY]
    falling = [after(v, lower_sum) for v in falling]
    falling = jnp.concatenate([falling[k][:, :half] for k in late], axis=2)
    from_above.append(permute(after(falling, lower_sum, column_labels, row_labels), down))

    one = ((0, 0),)
    ends = (blocks[last:], both[last:], half)
    near_below = [after(from_below[last], tiles[0], tiles[2])]
    tiles = tiles_of(near_below, one, *ends, near, spot, carry=lower_sum)
    near_held = reduce_x_y(tiles, inner[1], inner[3])
    far_below = [after(from_below[last], tiles[0], tiles[2])]
    far_held = reduce_x_y(tiles_of(far_below, one, *ends, far, spot, carry=lower_sum, skip=len(NEAR)), inner[1], inner[3])
    inner = reduce_y_x(*halve(*inner, spot))
    near_held = reduce_y_x(*halve(*near_held, spot))
    far_held = reduce_y_x(*halve(*far_held, spot))
    begins = {k: 2 * sum(chunks[i] for i in late if i < k) for k in late}
    starts = tuple((EARLY.index(k), 0) if k in EARLY else (len(EARLY), begins[k]) for k in range(len(chunks)))
    keep, *sends = tiles_of(from_above, starts, blocks, both, half, upper, spot, direct=True)
    upper_held = [keep] + [permute(v, swap(shape, m)) for m, v in enumerate(sends, 1)]
    sums = tally(inner, INNER, None)
    sums = tally(near_held, NEAR, sums)
    sums = tally(far_held, FAR, sums)
    sums = tally(upper_held, UPPER, sums)

    mine = sums[0]
    for m in range(1, GROUP):
        mine = mine + permute(sums[m], swap(shape, m))
    home = []
    for r in range(shape[0]):
        block = r % GROUP
        if block in (0, GROUP - 2, GROUP - 1):
            planes = 1 if block == 0 else -1
            home += [(r * 2 + c, (r + planes * GROUP) % shape[0] * 2 + c) for c in range(2)]
    mine = mine[:2] + permute(mine[2:4], home)
    return mine + permute(mine, across)


def solution(mesh):
    shape = (mesh.shape["rows"], mesh.shape["feat"])
    placed = (P("rows", "feat"), P("rows"), P("rows"))
    return jax.shard_map(
        functools.partial(local, shape), mesh=mesh, in_specs=placed, out_specs=P(None, "rows"), check_vma=False
    )
```
